256 devices in a mesh: dp: 16 (over y, x), opt: 16 (over z, core).
Axes of the slice: x: 4, y: 4, z: 8, core: 2. Of those that a mesh axis runs over, the one named last changes fastest.
Arguments:
- inputs: bfloat16 [2, 8192, 4096], P(None, 'dp'), may hold values from -6 to 6
- output_grads: bfloat16 [8192, 16384], P('dp', 'opt'), may hold values from -0.0625 to 0.0625
- owner_map: int32 [16, 16], P('dp'), may hold values from 0 to 15, as said below
- left_stats: bfloat16 [16, 16, 2, 512, 512], P('dp', 'opt'), may hold values from -10 to 40, as said below
- right_stats: bfloat16 [16, 16, 2, 512, 512], P('dp', 'opt'), may hold values from -10 to 40, as said below
- left_roots: bfloat16 [16, 16, 2, 512, 512], P('dp', 'opt'), may hold values from -4 to 10, as said below
- right_roots: bfloat16 [16, 16, 2, 512, 512], P('dp', 'opt'), may hold values from -4 to 10, as said below
Outputs:
- update: bfloat16 [16, 16, 512, 512], P('opt', 'dp')
- left_updated: bfloat16 [16, 16, 2, 512, 512], P('dp', 'opt')
- right_updated: bfloat16 [16, 16, 2, 512, 512], P('dp', 'opt')
The draws below stay inside these ranges and needn't reach their ends.
Inputs may be any that keep to these rules, and one draw needn't show every extreme that they name: `owner_map`: in every row each owner is named at most 2 times, and 4 owners are named exactly 2 times. `left_stats`: each block is symmetric. `right_stats`: each block is symmetric. `left_roots`: each block is symmetric. `right_roots`: each block is symmetric.
All inputs are finite; a program needn't handle non-finite values.
Results may differ from the reference program's by a relative error of at most 0.023.
Values may be sent and summed in bfloat16 or wider, within the bound.
No kernel may reach another device: no remote copies, remote signals or barrier semaphores. Data moves between devices by JAX's collectives and lax.ppermute only.
A program may use at most 128 MiB of HBM per device.

```python
import jax
import jax.numpy as jnp
from jax import lax

B = 512
CAP = 2
TOKENS = 8192
DWIN = 4096
DOUT = 4096
N_DP = 16
N_OPT = 16


def symmetric_blocks(key, lowest, highest, spread, top_scale):
    key_diag, key_off, key_scale = jax.random.split(key, 3)
    dims_shape = (N_DP, N_OPT, CAP, B, B)
    diagonal = jnp.exp(jax.random.uniform(key_diag, dims_shape[:-1], jnp.float32, jnp.log(lowest), jnp.log(highest)))
    off_part = jnp.clip(jax.random.normal(key_off, dims_shape, jnp.float32), -4.0, 4.0) * (spread / B ** 0.5)
    off_part = (off_part + jnp.swapaxes(off_part, -1, -2)) * 0.7071
    scales = jnp.exp(jax.random.uniform(key_scale, dims_shape[:-1], jnp.float32, 0.0, jnp.log(top_scale)))
    identity = jnp.eye(B, dtype=jnp.float32)
    whole = off_part + identity * diagonal[..., None]
    return whole * scales[..., :, None] * scales[..., None, :]


def draw_left_stats(key, part):
    key = jax.random.fold_in(key, 21)
    top_scale = 1.0
    return symmetric_blocks(key, 0.5, 2.0, 0.5, top_scale).astype(jnp.bfloat16)


def draw_right_stats(key, part):
    key = jax.random.fold_in(key, 22)
    top_scale = 1.0
    return symmetric_blocks(key, 0.5, 2.0, 0.5, top_scale).astype(jnp.bfloat16)


def draw_left_roots(key, part):
    key = jax.random.fold_in(key, 23)
    top_scale = 1.0
    return symmetric_blocks(key, 0.4, 1.5, 0.4, top_scale).astype(jnp.bfloat16)


def draw_right_roots(key, part):
    key = jax.random.fold_in(key, 24)
    top_scale = 1.0
    return symmetric_blocks(key, 0.4, 1.5, 0.4, top_scale).astype(jnp.bfloat16)


def draw_owner_map(key, part):
    key = jax.random.fold_in(key, 41)
    row_keys = jax.random.split(key, N_DP)
    quarter = N_OPT // 4
    places = jnp.arange(N_OPT, dtype=jnp.int32)

    def one_row(row_key):
        key_order, key_mix = jax.random.split(row_key)
        owner_order = jax.random.permutation(key_order, N_OPT)
        picked_slots = jnp.where(places < 2 * quarter, places // 2, places - quarter)
        listed = owner_order[picked_slots]
        return listed[jax.random.permutation(key_mix, N_OPT)].astype(jnp.int32)
    return jax.vmap(one_row)(row_keys)


def block_scale(key, dims, shards, least, largest):
    loudness = 1.0
    for dim, parts in shards:
        steps = jax.random.uniform(jax.random.fold_in(jax.random.fold_in(key, 6), dim), (parts,), jnp.float32, least / len(shards), largest / len(shards))
        loudness = loudness * jnp.repeat(jnp.exp(steps), dims[dim] // parts).reshape((-1,) + (1,) * (len(dims) - 1 - dim))
    return loudness


def normal_values(rng, extent, width, most, pieces=(), kind=jnp.bfloat16):
    values = jax.random.normal(rng, extent, jnp.float32) * width
    if len(pieces) > 0:
        values = block_scale(rng, extent, pieces, -0.22, 0.18) * values
    return jnp.clip(values, min=-most, max=most).astype(kind)


def setup_inputs(seed: int = 0) -> dict:
    seeds = jax.random.split(jax.random.key(seed), 8)
    return {
        "inputs": normal_values(seeds[0], (2, TOKENS, DWIN), 1.0, 6.0, ((1, 16),)),
        "output_grads": normal_values(seeds[1], (TOKENS, 4 * DOUT), TOKENS ** -0.5, 0.0625, ((0, 16), (1, 16))),
        "owner_map": draw_owner_map(jax.random.fold_in(seeds[7], 71), 0),
        "left_stats": draw_left_stats(jax.random.fold_in(seeds[7], 71), 0),
        "right_stats": draw_right_stats(jax.random.fold_in(seeds[7], 71), 0),
        "left_roots": draw_left_roots(jax.random.fold_in(seeds[7], 71), 0),
        "right_roots": draw_right_roots(jax.random.fold_in(seeds[7], 71), 0),
    }


DECAY_RATE = 0.95

def owner_ranks(owners):
    places = jnp.arange(owners.shape[0], dtype=jnp.int32)
    earlier = (owners[None, :] == owners[:, None]) & (places[None, :] < places[:, None])
    return lax.optimization_barrier(jnp.sum(earlier.astype(jnp.int32), axis=1)).astype(jnp.int32)

def reference(inputs, output_grads, owner_map, left_stats, right_stats, left_roots, right_roots):
    block_size = left_stats.shape[-1]
    tok_rows = inputs.shape[1] // N_DP
    col_width = output_grads.shape[1] // N_OPT
    col_blocks = col_width // block_size
    row_blocks = inputs.shape[2] // block_size
    grouped = inputs.reshape(2, N_DP, tok_rows, inputs.shape[2])
    targets = output_grads.reshape(N_DP, tok_rows, N_OPT, col_width)

    def shard_grad(shard_index):
        chooser = (shard_index * 4 // N_OPT == 3).astype(jnp.int32)
        source = lax.dynamic_index_in_dim(grouped, chooser, 0, keepdims=False)
        target = lax.dynamic_index_in_dim(targets, shard_index, 2, keepdims=False)
        partial_sums = jnp.einsum('gtb,gtc->gbc', source.astype(jnp.float32), target.astype(jnp.float32))
        rounded = lax.optimization_barrier(partial_sums.astype(jnp.bfloat16))
        summed = lax.optimization_barrier(jnp.sum(rounded.astype(jnp.float32), axis=0)).astype(jnp.bfloat16)
        tiled_grad = summed.reshape(row_blocks, block_size, col_blocks, block_size)
        return jnp.transpose(tiled_grad, (0, 2, 1, 3)).reshape(row_blocks * col_blocks, block_size, block_size)
    grads = lax.map(shard_grad, jnp.arange(N_OPT, dtype=jnp.int32))

    def dp_row(row_index):
        owners = owner_map[row_index]
        slot_ranks = owner_ranks(owners)
        blocks = lax.dynamic_index_in_dim(grads, row_index, 1, keepdims=False).astype(jnp.float32)
        gram_left = jnp.einsum('hij,hkj->hik', blocks, blocks) / block_size
        gram_right = jnp.einsum('hji,hjk->hik', blocks, blocks) / block_size
        left_row = lax.dynamic_index_in_dim(left_stats, row_index, 0, keepdims=False).astype(jnp.float32) * DECAY_RATE
        right_row = lax.dynamic_index_in_dim(right_stats, row_index, 0, keepdims=False).astype(jnp.float32) * DECAY_RATE
        left_row = left_row.at[owners, slot_ranks].add(gram_left)
        right_row = right_row.at[owners, slot_ranks].add(gram_right)
        left_root = lax.dynamic_index_in_dim(left_roots, row_index, 0, keepdims=False)[owners, slot_ranks].astype(jnp.float32)
        right_root = lax.dynamic_index_in_dim(right_roots, row_index, 0, keepdims=False)[owners, slot_ranks].astype(jnp.float32)
        twisted = lax.optimization_barrier(jnp.einsum('hij,hjk->hik', blocks, right_root).astype(jnp.bfloat16))
        result = jnp.einsum('hij,hjk->hik', left_root, twisted.astype(jnp.float32)).astype(jnp.bfloat16)
        return (left_row.astype(jnp.bfloat16), right_row.astype(jnp.bfloat16), result)
    left_updated, right_updated, results = lax.map(dp_row, jnp.arange(N_DP, dtype=jnp.int32))
    return (jnp.transpose(results, (1, 0, 2, 3)), left_updated, right_updated)
```

```python
import functools

import jax
import jax.numpy as jnp
from jax import lax
from jax.experimental import pallas as pl
from jax.experimental.pallas import tpu as pltpu
from jax.sharding import PartitionSpec as P

DECAY_RATE = 0.95
SIDE = 4
PAIRS = [(i, j) for i in range(4) for j in range(i, 4)]
VMEM_BYTES = 40 * 1024 * 1024
F32 = jnp.float32
BF16 = jnp.bfloat16


def params():
    return pltpu.CompilerParams(vmem_limit_bytes=VMEM_BYTES)


def cost(flops, moved):
    return pl.CostEstimate(flops=int(flops), bytes_accessed=int(moved), transcendentals=0)


def x_ring(step):
    return [(y * SIDE + x, y * SIDE + (x + step) % SIDE) for y in range(SIDE) for x in range(SIDE)]


def y_ring(step):
    return [(y * SIDE + x, ((y + step) % SIDE) * SIDE + x) for y in range(SIDE) for x in range(SIDE)]


def dot(a, b, over_a, over_b):
    return lax.dot_general(a, b, (((over_a,), (over_b,)), ((), ())), preferred_element_type=F32)


def partial_kernel(per_out, feats, cols, chooser, *refs):
    count = len(refs) - 1
    n_out = count // (per_out + 1)
    sources, target, outs = refs[: n_out * per_out], refs[n_out * per_out], refs[n_out * per_out + 1 :]
    block = outs[0].shape[-1]
    for o in range(n_out):
        for t in range(per_out):
            u = o * per_out + t
            start = pl.multiple_of(cols[u] * block, block)
            rhs = target[:, pl.ds(start, block)]
            outs[o][t] = dot(sources[u][...], rhs, 0, 0).astype(BF16)


def partials(inputs, output_grads, chooser, feats, cols, per_out, block):
    units = feats.shape[0]
    tok, half = inputs.shape[1], block // 2
    n_out = units // per_out

    def source_spec(u):
        return pl.BlockSpec((None, tok, half), lambda i, f, c, w: (w[0], 0, f[u]))

    out_spec = pl.BlockSpec((per_out, half, block), lambda i, f, c, w: (0, 0, 0))
    return pl.pallas_call(
        functools.partial(partial_kernel, per_out),
        grid_spec=pltpu.PrefetchScalarGridSpec(
            num_scalar_prefetch=3,
            grid=(1,),
            in_specs=[source_spec(u) for u in range(units)]
            + [pl.BlockSpec(output_grads.shape, lambda i, f, c, w: (0, 0))],
            out_specs=[out_spec] * n_out,
        ),
        out_shape=[jax.ShapeDtypeStruct((per_out, half, block), BF16)] * n_out,
        compiler_params=params(),
        cost_estimate=cost(
            2 * units * tok * half * block,
            2 * (units * tok * half + output_grads.size + units * half * block),
        ),
        name="partials",
    )(feats, cols, chooser, *([inputs] * units), output_grads)


def pieces(quarter, parts):
    rows = len(PAIRS) * quarter // parts
    for j in range(parts):
        at = j * rows
        while at < (j + 1) * rows:
            p, r = divmod(at, quarter)
            n = min(quarter - r, (j + 1) * rows - at)
            yield j, at - j * rows, n, PAIRS[p], r
            at += n


def pack_kernel(left, right, out):
    quarter = left.shape[-1] // 4
    for c in range(left.shape[0]):
        for m, ref in enumerate((left, right)):
            for j, at, n, (bi, bj), r in pieces(quarter, out.shape[0]):
                out[j, 2 * c + m, at : at + n, :] = ref[
                    c, bi * quarter + r : bi * quarter + r + n, bj * quarter : (bj + 1) * quarter
                ]


def pack_roots(left, right, parts):
    cap, block = left.shape[0], left.shape[-1]
    quarter = block // 4
    shape = (parts, 2 * cap, len(PAIRS) * quarter // parts, quarter)
    return pl.pallas_call(
        pack_kernel,
        out_shape=jax.ShapeDtypeStruct(shape, BF16),
        compiler_params=params(),
        cost_estimate=cost(0, 3 * 2 * left.size),
        name="pack_roots",
    )(left, right)


def pick_kernel(index, src, out):
    for i in range(out.shape[0]):
        at = index[i]

        @pl.when(at >= 0)
        def _(i=i, at=at):
            out[i] = src[jnp.maximum(at, 0)]

        @pl.when(at < 0)
        def _(i=i):
            out[i] = jnp.zeros(out.shape[1:], out.dtype)


def pick(index, src):
    shape = (index.shape[0],) + src.shape[1:]
    return pl.pallas_call(
        pick_kernel,
        in_specs=[pl.BlockSpec(memory_space=pltpu.SMEM), pl.BlockSpec(memory_space=pltpu.VMEM)],
        out_specs=pl.BlockSpec(memory_space=pltpu.VMEM),
        out_shape=jax.ShapeDtypeStruct(shape, src.dtype),
        compiler_params=params(),
        cost_estimate=cost(0, 4 * src.size),
        name="pick",
    )(index, src)


def unpack_kernel(packed, out):
    quarter = out.shape[-1] // 4
    for m in range(2):
        for j, at, n, (bi, bj), r in pieces(quarter, packed.shape[0]):
            out[m, bi * quarter + r : bi * quarter + r + n, bj * quarter : (bj + 1) * quarter] = packed[
                j, m, at : at + n, :
            ]
        for bi, bj in PAIRS:
            if bi != bj:
                out[m, bj * quarter : (bj + 1) * quarter, bi * quarter : (bi + 1) * quarter] = out[
                    m, bi * quarter : (bi + 1) * quarter, bj * quarter : (bj + 1) * quarter
                ].T


def unpack_roots(packed, block):
    return pl.pallas_call(
        unpack_kernel,
        out_shape=jax.ShapeDtypeStruct((2, block, block), BF16),
        compiler_params=params(),
        cost_estimate=cost(0, 8 * block * block),
        name="unpack_roots",
    )(packed)


def update_kernel(roots, grad, out):
    twisted = dot(grad[...], roots[1], 1, 0).astype(BF16)
    out[...] = dot(roots[0], twisted, 1, 0).astype(BF16)


def precondition(roots, grad):
    block = grad.shape[-1]
    return pl.pallas_call(
        update_kernel,
        out_shape=jax.ShapeDtypeStruct(grad.shape, BF16),
        compiler_params=params(),
        cost_estimate=cost(4 * block**3, 8 * block * block),
        name="precondition",
    )(roots, grad)


def gram_kernel(grads, left, right, left_out, right_out):
    block = left.shape[-1]
    grad = grads[...].reshape(block, block)
    gram = dot(grad, grad, 1, 1)
    left_out[...] = (left[...].astype(F32) * DECAY_RATE + gram / block).astype(BF16)
    gram = dot(grad, grad, 0, 0)
    right_out[...] = (right[...].astype(F32) * DECAY_RATE + gram / block).astype(BF16)


def grams(grads, left, right):
    parts, cap, rows, block = grads.shape
    stat = pl.BlockSpec((None, block, block), lambda c: (c, 0, 0))
    return pl.pallas_call(
        gram_kernel,
        grid=(cap,),
        in_specs=[pl.BlockSpec((parts, None, rows, block), lambda c: (0, c, 0, 0)), stat, stat],
        out_specs=[stat, stat],
        out_shape=[jax.ShapeDtypeStruct(left.shape, BF16)] * 2,
        compiler_params=params(),
        cost_estimate=cost(4 * cap * block**3, 10 * cap * block * block),
        name="grams",
    )(grads, left, right)


def total(*terms):
    return functools.reduce(jnp.add, [t.astype(F32) for t in terms]).astype(BF16)


def shards(inputs, output_grads, owner_map, left_stats, right_stats, left_roots, right_roots):
    block = left_stats.shape[-1]
    cap = left_stats.shape[2]
    col_blocks = output_grads.shape[1] // block
    opt_count = lax.axis_size("opt")
    shard = lax.axis_index("opt")
    home = lax.axis_index("dp")
    y, x = home // SIDE, home % SIDE
    chooser = (shard * 4 // opt_count == 3).astype(jnp.int32).reshape(1)

    owners = owner_map[0]
    places = jnp.arange(opt_count, dtype=jnp.int32)
    same = (owners[None, :] == owners[:, None]) & (places[None, :] < places[:, None])
    slots = owners * cap + jnp.sum(same.astype(jnp.int32), axis=1)
    slot_ids = jnp.arange(opt_count * cap, dtype=jnp.int32)
    holders = slots[None, :] == slot_ids[:, None]
    homes = jnp.sum(jnp.where(holders, places[None, :] + 1, 0), axis=1) - 1

    lanes = jnp.arange(SIDE, dtype=jnp.int32)

    def unit_places(steps, along_x):
        feats, cols = [], []
        for r in steps:
            if along_x:
                k = ((y + lanes) % SIDE) * SIDE + (x + r) % SIDE
                feats.append((k // col_blocks) * 2)
            else:
                k = ((y + r) % SIDE) * SIDE + (x + lanes) % SIDE
                feats.append((k // col_blocks) * 2 + 1)
            cols.append(k % col_blocks)
        return feats, cols

    def chunks(steps):
        fa, ca = unit_places(steps, True)
        fb, cb = unit_places(steps, False)
        return partials(
            inputs, output_grads, chooser, jnp.concatenate(fa + fb), jnp.concatenate(ca + cb), 2, block
        )

    a2l, a2h, b2l, b2h = chunks((2,))
    a1l, a1h, a3l, a3h, b1l, b1h, b3l, b3h = chunks((1, 3))
    a0l, a0h, b0l, b0h = chunks((0,))

    right, left = x_ring(1), x_ring(-1)
    down, up = y_ring(1), y_ring(-1)

    def send(value, ring):
        return lax.ppermute(value, "dp", ring)

    packed = pack_roots(left_roots[0, 0], right_roots[0, 0], opt_count)

    a_r1, a_l1 = send(a2l, right), send(a2h, left)
    b_r1, b_l1 = send(b2l, down), send(b2h, up)
    a_r2, a_l2 = send(a1h, right), send(a3l, left)
    b_r2, b_l2 = send(b1h, down), send(b3l, up)

    spread = lax.all_to_all(packed, "opt", 0, 0, tiled=True)

    a_r3, a_l3 = send(total(a1l, a_r1), right), send(total(a3h, a_l1), left)
    b_r3, b_l3 = send(total(b1l, b_r1), down), send(total(b3h, b_l1), up)

    chosen = pick(slots, spread.reshape((opt_count * cap, 2) + spread.shape[2:]))
    gathered = lax.all_to_all(chosen, "opt", 0, 0, tiled=True)
    roots = unpack_roots(gathered, block)

    al, ah = total(a0l, a_r3, a_l2), total(a0h, a_r2, a_l3)
    bl, bh = total(b0l, b_r3, b_l2), total(b0h, b_r2, b_l3)

    part = block // 4
    a_r1, a_l1 = send(ah[0, :part], down), send(ah[0, part:], up)
    b_r1, b_l1 = send(bh[0, :part], right), send(bh[0, part:], left)

    def joined(own, first, last):
        top = own[:part] if first is None else total(own[:part], first)
        rest = own[part:] if last is None else total(own[part:], last)
        return jnp.concatenate([top, rest], axis=0)

    a_r2, a_l2 = send(joined(al[1], a_r1, None), down), send(joined(ah[1], None, a_l1), up)
    b_r2, b_l2 = send(joined(bl[1], b_r1, None), right), send(joined(bh[1], None, b_l1), left)
    grad = jnp.concatenate([total(al[0], a_r2, a_l2), total(bl[0], b_r2, b_l2)], axis=0)

    rows = block // opt_count
    spread = lax.all_to_all(grad.reshape(opt_count, rows, block), "opt", 0, 0, tiled=True)
    chosen = pick(homes, spread).reshape(opt_count, cap, rows, block)
    owned = lax.all_to_all(chosen, "opt", 0, 0, tiled=True)
    update = precondition(roots, grad)
    left_updated, right_updated = grams(owned, left_stats[0, 0], right_stats[0, 0])
    return update[None, None], left_updated[None, None], right_updated[None, None]


def solution(mesh):
    return jax.shard_map(
        shards,
        mesh=mesh,
        in_specs=(
            P(None, "dp", None),
            P("dp", "opt"),
            P("dp", None),
            P("dp", "opt", None, None, None),
            P("dp", "opt", None, None, None),
            P("dp", "opt", None, None, None),
            P("dp", "opt", None, None, None),
        ),
        out_specs=(
            P("opt", "dp", None, None),
            P("dp", "opt", None, None, None),
            P("dp", "opt", None, None, None),
        ),
        check_vma=False,
    )
```

```python
import functools

import jax
import jax.numpy as jnp
from jax import lax
from jax.experimental import pallas as pl
from jax.experimental.pallas import tpu as pltpu
from jax.sharding import PartitionSpec as P

DECAY_RATE = 0.95
SIDE = 4
OFF = [(i, j) for i in range(4) for j in range(i + 1, 4)]
VMEM_BYTES = 32 * 1024 * 1024
VMEM_PARTIALS = 60 * 1024 * 1024
F32 = jnp.float32
BF16 = jnp.bfloat16


def params(limit=VMEM_BYTES):
    return pltpu.CompilerParams(vmem_limit_bytes=limit)


def cost(flops, moved):
    return pl.CostEstimate(flops=int(flops), bytes_accessed=int(moved), transcendentals=0)


def x_ring(step):
    return [(y * SIDE + x, y * SIDE + (x + step) % SIDE) for y in range(SIDE) for x in range(SIDE)]


def y_ring(step):
    return [(y * SIDE + x, ((y + step) % SIDE) * SIDE + x) for y in range(SIDE) for x in range(SIDE)]


def dot(a, b, over_a, over_b):
    return lax.dot_general(a, b, (((over_a,), (over_b,)), ((), ())), preferred_element_type=F32)


def partial_kernel(per_out, feats, cols, chooser, *refs):
    count = len(refs) - 1
    n_out = count // (per_out + 1)
    sources, target, outs = refs[: n_out * per_out], refs[n_out * per_out], refs[n_out * per_out + 1 :]
    block = outs[0].shape[-1]
    for o in range(n_out):
        for t in range(per_out):
            u = o * per_out + t
            start = pl.multiple_of(cols[u] * block, block)
            rhs = target[:, pl.ds(start, block)]
            outs[o][t] = dot(sources[u][...], rhs, 0, 0).astype(BF16)


def partials(inputs, output_grads, chooser, feats, cols, per_out, block):
    units = feats.shape[0]
    tok, half = inputs.shape[1], block // 2
    n_out = units // per_out

    def source_spec(u):
        return pl.BlockSpec((None, tok, half), lambda i, f, c, w: (w[0], 0, f[u]))

    out_spec = pl.BlockSpec((per_out, half, block), lambda i, f, c, w: (0, 0, 0))
    return pl.pallas_call(
        functools.partial(partial_kernel, per_out),
        grid_spec=pltpu.PrefetchScalarGridSpec(
            num_scalar_prefetch=3,
            grid=(1,),
            in_specs=[source_spec(u) for u in range(units)]
            + [pl.BlockSpec(output_grads.shape, lambda i, f, c, w: (0, 0))],
            out_specs=[out_spec] * n_out,
        ),
        out_shape=[jax.ShapeDtypeStruct((per_out, half, block), BF16)] * n_out,
        compiler_params=params(VMEM_PARTIALS),
        cost_estimate=cost(
            2 * units * tok * half * block,
            2 * (units * tok * half + output_grads.size + units * half * block),
        ),
        name="partials",
    )(feats, cols, chooser, *([inputs] * units), output_grads)


def grid_masks(n):
    rows = lax.broadcasted_iota(jnp.int32, (n, n), 0)
    cols = lax.broadcasted_iota(jnp.int32, (n, n), 1)
    return rows, cols


def pack_kernel(left, right, out, diag):
    q = left.shape[-1] // 4
    parts = out.shape[0]
    per = parts // 8
    rows, cols = grid_masks(q)
    diag[...] = jnp.zeros(diag.shape, diag.dtype)

    def put(slot, piece, value):
        step = q // per
        for h in range(per):
            out[piece * per + h, slot] = value[h * step : (h + 1) * step]

    for c in range(left.shape[0]):
        for m, ref in enumerate((left, right)):

            def quarter(i, j, ref=ref, c=c):
                return ref[c, i * q : (i + 1) * q, j * q : (j + 1) * q]

            for n, (i, j) in enumerate(OFF):
                put(2 * c + m, n, quarter(i, j))
            for h in range(2):
                upper, lower = quarter(2 * h, 2 * h), quarter(2 * h + 1, 2 * h + 1)
                put(2 * c + m, len(OFF) + h, jnp.where(rows <= cols, upper, lower))
                line = jnp.sum(jnp.where(rows == cols, lower.astype(F32), 0.0), axis=0, keepdims=True)
                diag[c, 2 * m + h : 2 * m + h + 1, :] = line


def pack_roots(left, right, parts):
    cap, block = left.shape[0], left.shape[-1]
    q = block // 4
    shape = (parts, 2 * cap, 8 * q // parts, q)
    return pl.pallas_call(
        pack_kernel,
        out_shape=[jax.ShapeDtypeStruct(shape, BF16), jax.ShapeDtypeStruct((cap, 8, q), F32)],
        compiler_params=params(),
        cost_estimate=cost(0, 3 * 2 * left.size),
        name="pack_roots",
    )(left, right)


def pick_kernel(index, src, out):
    for i in range(out.shape[0]):
        at = index[i]

        @pl.when(at >= 0)
        def _(i=i, at=at):
            out[i] = src[jnp.maximum(at, 0)]

        @pl.when(at < 0)
        def _(i=i):
            out[i] = jnp.zeros(out.shape[1:], out.dtype)


def pick(index, src):
    shape = (index.shape[0],) + src.shape[1:]
    return pl.pallas_call(
        pick_kernel,
        in_specs=[pl.BlockSpec(memory_space=pltpu.SMEM), pl.BlockSpec(memory_space=pltpu.VMEM)],
        out_specs=pl.BlockSpec(memory_space=pltpu.VMEM),
        out_shape=jax.ShapeDtypeStruct(shape, src.dtype),
        compiler_params=params(),
        cost_estimate=cost(0, 4 * src.size),
        name="pick",
    )(index, src)


def unpack_kernel(slot, packed, diag, out):
    q = out.shape[-1] // 4
    per = packed.shape[0] // 8
    rows, cols = grid_masks(q)
    line = diag[slot[0]]
    for m in range(2):

        def piece(n, m=m):
            return jnp.concatenate([packed[n * per + h, m] for h in range(per)], axis=0)

        def put(i, j, value, m=m):
            out[m, i * q : (i + 1) * q, j * q : (j + 1) * q] = value

        for n, (i, j) in enumerate(OFF):
            value = piece(n)
            put(i, j, value)
            put(j, i, value.T)
        for h in range(2):
            value = piece(len(OFF) + h)
            turned = value.T
            put(2 * h, 2 * h, jnp.where(rows <= cols, value, turned))
            own = jnp.broadcast_to(line[2 * m + h : 2 * m + h + 1, :], (q, q)).astype(BF16)
            lower = jnp.where(rows > cols, value, turned)
            put(2 * h + 1, 2 * h + 1, jnp.where(rows == cols, own, lower))


def unpack_roots(slot, packed, diag, block):
    return pl.pallas_call(
        unpack_kernel,
        in_specs=[pl.BlockSpec(memory_space=pltpu.SMEM)] + [pl.BlockSpec(memory_space=pltpu.VMEM)] * 2,
        out_specs=pl.BlockSpec(memory_space=pltpu.VMEM),
        out_shape=jax.ShapeDtypeStruct((2, block, block), BF16),
        compiler_params=params(),
        cost_estimate=cost(0, 8 * block * block),
        name="unpack_roots",
    )(slot, packed, diag)


def update_kernel(roots, grad, out):
    twisted = dot(grad[...], roots[1], 1, 0).astype(BF16)
    out[...] = dot(roots[0], twisted, 1, 0).astype(BF16)


def precondition(roots, grad):
    block = grad.shape[-1]
    return pl.pallas_call(
        update_kernel,
        out_shape=jax.ShapeDtypeStruct(grad.shape, BF16),
        compiler_params=params(),
        cost_estimate=cost(4 * block**3, 8 * block * block),
        name="precondition",
    )(roots, grad)


def gram_kernel(grads, left, right, left_out, right_out):
    block = left.shape[-1]
    grad = grads[...].reshape(block, block)
    gram = dot(grad, grad, 1, 1)
    left_out[...] = (left[...].astype(F32) * DECAY_RATE + gram / block).astype(BF16)
    gram = dot(grad, grad, 0, 0)
    right_out[...] = (right[...].astype(F32) * DECAY_RATE + gram / block).astype(BF16)


def grams(grads, left, right):
    parts, cap, rows, block = grads.shape
    stat = pl.BlockSpec((None, block, block), lambda c: (c, 0, 0))
    return pl.pallas_call(
        gram_kernel,
        grid=(cap,),
        in_specs=[pl.BlockSpec((parts, None, rows, block), lambda c: (0, c, 0, 0)), stat, stat],
        out_specs=[stat, stat],
        out_shape=[jax.ShapeDtypeStruct(left.shape, BF16)] * 2,
        compiler_params=params(),
        cost_estimate=cost(4 * cap * block**3, 10 * cap * block * block),
        name="grams",
    )(grads, left, right)


def total(*terms):
    return functools.reduce(jnp.add, [t.astype(F32) for t in terms]).astype(BF16)


def shards(inputs, output_grads, owner_map, left_stats, right_stats, left_roots, right_roots):
    block = left_stats.shape[-1]
    cap = left_stats.shape[2]
    col_blocks = output_grads.shape[1] // block
    opt_count = lax.axis_size("opt")
    shard = lax.axis_index("opt")
    home = lax.axis_index("dp")
    y, x = home // SIDE, home % SIDE
    chooser = (shard * 4 // opt_count == 3).astype(jnp.int32).reshape(1)

    owners = owner_map[0]
    places = jnp.arange(opt_count, dtype=jnp.int32)
    same = (owners[None, :] == owners[:, None]) & (places[None, :] < places[:, None])
    slots = owners * cap + jnp.sum(same.astype(jnp.int32), axis=1)
    slot_ids = jnp.arange(opt_count * cap, dtype=jnp.int32)
    holders = slots[None, :] == slot_ids[:, None]
    homes = jnp.sum(jnp.where(holders, places[None, :] + 1, 0), axis=1) - 1

    lanes = jnp.arange(SIDE, dtype=jnp.int32)

    def unit_places(steps, along_x):
        feats, cols = [], []
        for r in steps:
            if along_x:
                k = ((y + lanes) % SIDE) * SIDE + (x + r) % SIDE
                feats.append((k // col_blocks) * 2)
            else:
                k = ((y + r) % SIDE) * SIDE + (x + lanes) % SIDE
                feats.append((k // col_blocks) * 2 + 1)
            cols.append(k % col_blocks)
        return feats, cols

    def chunks(steps, per_out, chooser):
        fa, ca = unit_places(steps, True)
        fb, cb = unit_places(steps, False)
        return partials(
            inputs, output_grads, chooser, jnp.concatenate(fa + fb), jnp.concatenate(ca + cb), per_out, block
        )

    a2l, a2h, b2l, b2h = chunks((2,), 2, chooser)
    a1, a3, b1, b3 = chunks((1, 3), 4, chooser)

    right, left = x_ring(1), x_ring(-1)
    down, up = y_ring(1), y_ring(-1)

    def send(value, ring):
        return lax.ppermute(value, "dp", ring)

    def joined(own, first, last):
        part = own.shape[0] // 2
        top = own[:part] if first is None else total(own[:part], first)
        rest = own[part:] if last is None else total(own[part:], last)
        return jnp.concatenate([top, rest], axis=0)

    packed, diag = pack_roots(left_roots[0, 0], right_roots[0, 0], opt_count)

    a_r1, a_l1 = send(a2l, right), send(a2h, left)
    b_r1, b_l1 = send(b2l, down), send(b2h, up)

    spread = lax.all_to_all(packed, "opt", 0, 0, tiled=True)
    diags = lax.all_gather(diag, "opt", axis=0, tiled=True)
    a0, b0 = chunks((0,), 4, lax.optimization_barrier((chooser, diags))[0])

    a_r2, a_l2 = send(joined(a1, a_r1, None), right), send(joined(a3, None, a_l1), left)
    b_r2, b_l2 = send(joined(b1, b_r1, None), down), send(joined(b3, None, b_l1), up)

    chosen = pick(slots, spread.reshape((opt_count * cap, 2) + spread.shape[2:]))
    gathered = lax.all_to_all(chosen, "opt", 0, 0, tiled=True)
    roots = unpack_roots(lax.dynamic_slice(slots, (shard,), (1,)), gathered, diags, block)

    a0, b0, chosen = lax.optimization_barrier((a0, b0, chosen))
    a_sum, b_sum = total(a0, a_r2, a_l2), total(b0, b_r2, b_l2)

    part = block // 4
    a_r1, a_l1 = send(a_sum[2, :part], down), send(a_sum[2, part:], up)
    b_r1, b_l1 = send(b_sum[2, :part], right), send(b_sum[2, part:], left)
    a_r2, a_l2 = send(joined(a_sum[1], a_r1, None), down), send(joined(a_sum[3], None, a_l1), up)
    b_r2, b_l2 = send(joined(b_sum[1], b_r1, None), right), send(joined(b_sum[3], None, b_l1), left)
    grad = jnp.concatenate([total(a_sum[0], a_r2, a_l2), total(b_sum[0], b_r2, b_l2)], axis=0)
    grad, roots = lax.optimization_barrier((grad, roots))

    rows = block // opt_count
    spread = lax.all_to_all(grad.reshape(opt_count, rows, block), "opt", 0, 0, tiled=True)
    picked = pick(homes, spread).reshape(opt_count, cap, rows, block)
    owned = lax.all_to_all(picked, "opt", 0, 0, tiled=True)
    update = precondition(roots, grad)
    left_updated, right_updated = grams(owned, left_stats[0, 0], right_stats[0, 0])
    return update[None, None], left_updated[None, None], right_updated[None, None]


def solution(mesh):
    return jax.shard_map(
        shards,
        mesh=mesh,
        in_specs=(
            P(None, "dp", None),
            P("dp", "opt"),
            P("dp", None),
            P("dp", "opt", None, None, None),
            P("dp", "opt", None, None, None),
            P("dp", "opt", None, None, None),
            P("dp", "opt", None, None, None),
        ),
        out_specs=(
            P("opt", "dp", None, None),
            P("dp", "opt", None, None, None),
            P("dp", "opt", None, None, None),
        ),
        check_vma=False,
    )
```

```python
import functools

import jax
import jax.numpy as jnp
from jax import lax
from jax.experimental import pallas as pl
from jax.experimental.pallas import tpu as pltpu
from jax.sharding import PartitionSpec as P

DECAY_RATE = 0.95
SIDE = 4
OFF = [(i, j) for i in range(4) for j in range(i + 1, 4)]
VMEM_BYTES = 32 * 1024 * 1024
VMEM_PARTIALS = 60 * 1024 * 1024
EXTRA = 16
F32 = jnp.float32
BF16 = jnp.bfloat16


def params(limit=VMEM_BYTES):
    return pltpu.CompilerParams(vmem_limit_bytes=limit)


def cost(flops, moved):
    return pl.CostEstimate(flops=int(flops), bytes_accessed=int(moved), transcendentals=0)


def x_ring(step):
    return [(y * SIDE + x, y * SIDE + (x + step) % SIDE) for y in range(SIDE) for x in range(SIDE)]


def y_ring(step):
    return [(y * SIDE + x, ((y + step) % SIDE) * SIDE + x) for y in range(SIDE) for x in range(SIDE)]


def dot(a, b, over_a, over_b):
    return lax.dot_general(a, b, (((over_a,), (over_b,)), ((), ())), preferred_element_type=F32)


def unit_place(step, chunks, first, col_blocks, y, x):
    chunk, t = lax.div(step, SIDE), lax.rem(step, SIDE)
    r = first + 2 * lax.rem(chunk, chunks // 2)
    along_x = chunk < chunks // 2
    k_y = lax.rem(y + jnp.where(along_x, t, r), SIDE)
    k_x = lax.rem(x + jnp.where(along_x, r, t), SIDE)
    k = k_y * SIDE + k_x
    return 2 * lax.div(k, col_blocks) + jnp.where(along_x, 0, 1), lax.rem(k, col_blocks)


def partial_kernel(per_out, chunks, first, col_blocks, place, source, target, *outs):
    step = pl.program_id(0)
    block = outs[0].shape[-1]
    _, col = unit_place(step, chunks, first, col_blocks, place[1], place[2])
    rhs = target[:, pl.ds(pl.multiple_of(col * block, block), block)]
    value = dot(source[...], rhs, 0, 0).astype(BF16)
    for o, out in enumerate(outs):

        @pl.when(lax.div(step, per_out) == o)
        def _(out=out):
            out[0] = value


def partials(inputs, output_grads, place, chunks, first, per_out, block):
    tok, half = inputs.shape[1], block // 2
    col_blocks = output_grads.shape[1] // block
    units = chunks * SIDE
    n_out = units // per_out

    def source_at(i, p):
        return p[0], 0, unit_place(i, chunks, first, col_blocks, p[1], p[2])[0]

    def out_spec(o):
        return pl.BlockSpec((1, half, block), lambda i, p: (jnp.clip(i - o * per_out, 0, per_out - 1), 0, 0))

    return pl.pallas_call(
        functools.partial(partial_kernel, per_out, chunks, first, col_blocks),
        grid_spec=pltpu.PrefetchScalarGridSpec(
            num_scalar_prefetch=1,
            grid=(units,),
            in_specs=[
                pl.BlockSpec((None, tok, half), source_at),
                pl.BlockSpec(output_grads.shape, lambda i, p: (0, 0)),
            ],
            out_specs=[out_spec(o) for o in range(n_out)],
        ),
        out_shape=[jax.ShapeDtypeStruct((per_out, half, block), BF16)] * n_out,
        compiler_params=params(VMEM_PARTIALS),
        cost_estimate=cost(
            2 * units * tok * half * block,
            2 * (units * tok * half + output_grads.size + units * half * block),
        ),
        name="partials",
    )(place, inputs, output_grads)


def grid_masks(n):
    rows = lax.broadcasted_iota(jnp.int32, (n, n), 0)
    cols = lax.broadcasted_iota(jnp.int32, (n, n), 1)
    return rows, cols


def pack_kernel(left, right, out):
    q = left.shape[-1] // 4
    parts = out.shape[0]
    per = parts // 8
    step = q // per
    rows, cols = grid_masks(q)

    def put(slot, piece, value):
        for h in range(per):
            out[piece * per + h, slot * step : (slot + 1) * step] = value[h * step : (h + 1) * step]

    lines = []
    for c in range(left.shape[0]):
        for m, ref in enumerate((left, right)):

            def quarter(i, j, ref=ref, c=c):
                return ref[c, i * q : (i + 1) * q, j * q : (j + 1) * q]

            for n, (i, j) in enumerate(OFF):
                put(2 * c + m, n, quarter(i, j))
            for h in range(2):
                upper, lower = quarter(2 * h, 2 * h), quarter(2 * h + 1, 2 * h + 1)
                put(2 * c + m, len(OFF) + h, jnp.where(rows <= cols, upper, lower))
                lines.append(jnp.sum(jnp.where(rows == cols, lower.astype(F32), 0.0), axis=0, keepdims=True))
    lines.append(jnp.zeros((EXTRA - len(lines), q), F32))
    extra = jnp.concatenate(lines, axis=0).astype(BF16)
    for j in range(parts):
        out[j, 2 * left.shape[0] * step :] = extra


def pack_roots(left, right, parts):
    cap, block = left.shape[0], left.shape[-1]
    q = block // 4
    shape = (parts, 2 * cap * (8 * q // parts) + EXTRA, q)
    return pl.pallas_call(
        pack_kernel,
        out_shape=jax.ShapeDtypeStruct(shape, BF16),
        compiler_params=params(),
        cost_estimate=cost(0, 3 * 2 * left.size),
        name="pack_roots",
    )(left, right)


def pick_roots_kernel(slots, src, out):
    body = out.shape[1] - EXTRA
    cap = (src.shape[1] - EXTRA) // body
    for i in range(out.shape[0]):
        owner, rank = lax.div(slots[i], cap), lax.rem(slots[i], cap)
        out[i, :body] = src[owner, pl.ds(pl.multiple_of(rank * body, body), body)]
        out[i, body:] = src[owner, cap * body :]


def pick_roots(slots, src, cap):
    rows = (src.shape[1] - EXTRA) // cap + EXTRA
    return pl.pallas_call(
        pick_roots_kernel,
        in_specs=[pl.BlockSpec(memory_space=pltpu.SMEM), pl.BlockSpec(memory_space=pltpu.VMEM)],
        out_specs=pl.BlockSpec(memory_space=pltpu.VMEM),
        out_shape=jax.ShapeDtypeStruct((slots.shape[0], rows, src.shape[2]), src.dtype),
        compiler_params=params(),
        cost_estimate=cost(0, 4 * src.size),
        name="pick_roots",
    )(slots, src)


def pick_kernel(index, src, out):
    for i in range(out.shape[0]):
        at = index[i]

        @pl.when(at >= 0)
        def _(i=i, at=at):
            out[i] = src[jnp.maximum(at, 0)]

        @pl.when(at < 0)
        def _(i=i):
            out[i] = jnp.zeros(out.shape[1:], out.dtype)


def pick(index, src):
    shape = (index.shape[0],) + src.shape[1:]
    return pl.pallas_call(
        pick_kernel,
        in_specs=[pl.BlockSpec(memory_space=pltpu.SMEM), pl.BlockSpec(memory_space=pltpu.VMEM)],
        out_specs=pl.BlockSpec(memory_space=pltpu.VMEM),
        out_shape=jax.ShapeDtypeStruct(shape, src.dtype),
        compiler_params=params(),
        cost_estimate=cost(0, 4 * src.size),
        name="pick",
    )(index, src)


def unpack_kernel(ranks, packed, out):
    q = out.shape[-1] // 4
    per = packed.shape[0] // 8
    step = q // per
    rows, cols = grid_masks(q)
    rank = ranks[0]
    lines = packed[0, 2 * step :].astype(F32)
    for m in range(2):

        def piece(n, m=m):
            return jnp.concatenate([packed[n * per + h, m * step : (m + 1) * step] for h in range(per)], axis=0)

        def put(i, j, value, m=m):
            out[m, i * q : (i + 1) * q, j * q : (j + 1) * q] = value

        for n, (i, j) in enumerate(OFF):
            value = piece(n)
            put(i, j, value)
            put(j, i, value.T)
        for h in range(2):
            value = piece(len(OFF) + h)
            turned = value.T
            put(2 * h, 2 * h, jnp.where(rows <= cols, value, turned))
            own = lines[2 * m + h : 2 * m + h + 1, :]
            for c in range(1, (EXTRA // 4)):
                at = 4 * c + 2 * m + h
                own = jnp.where(rank == c, lines[at : at + 1, :], own)
            own = jnp.broadcast_to(own, (q, q)).astype(BF16)
            lower = jnp.where(rows > cols, value, turned)
            put(2 * h + 1, 2 * h + 1, jnp.where(rows == cols, own, lower))


def unpack_roots(rank, packed, block):
    return pl.pallas_call(
        unpack_kernel,
        in_specs=[pl.BlockSpec(memory_space=pltpu.SMEM), pl.BlockSpec(memory_space=pltpu.VMEM)],
        out_specs=pl.BlockSpec(memory_space=pltpu.VMEM),
        out_shape=jax.ShapeDtypeStruct((2, block, block), BF16),
        compiler_params=params(),
        cost_estimate=cost(0, 8 * block * block),
        name="unpack_roots",
    )(rank, packed)


def update_kernel(roots, upper, lower, out):
    half = upper.shape[0]
    twisted = [dot(part[...], roots[1], 1, 0).astype(BF16) for part in (upper, lower)]
    out[...] = (dot(roots[0, :, :half], twisted[0], 1, 0) + dot(roots[0, :, half:], twisted[1], 1, 0)).astype(BF16)


def precondition(roots, upper, lower):
    block = upper.shape[-1]
    return pl.pallas_call(
        update_kernel,
        out_shape=jax.ShapeDtypeStruct((block, block), BF16),
        compiler_params=params(),
        cost_estimate=cost(4 * block**3, 8 * block * block),
        name="precondition",
    )(roots, upper, lower)


def gram_kernel(upper, lower, left, right, left_out, right_out):
    block = left.shape[-1]
    half = block // 2
    parts = [part[...].reshape(half, block) for part in (upper, lower)]
    for i in range(2):
        for j in range(2):
            at = slice(i * half, (i + 1) * half), slice(j * half, (j + 1) * half)
            gram = dot(parts[i], parts[j], 1, 1)
            left_out[at] = (left[at].astype(F32) * DECAY_RATE + gram / block).astype(BF16)
    gram = dot(parts[0], parts[0], 0, 0) + dot(parts[1], parts[1], 0, 0)
    right_out[...] = (right[...].astype(F32) * DECAY_RATE + gram / block).astype(BF16)


def grams(upper, lower, left, right):
    parts, cap, rows, block = upper.shape
    stat = pl.BlockSpec((None, block, block), lambda c: (c, 0, 0))
    half = pl.BlockSpec((parts, None, rows, block), lambda c: (0, c, 0, 0))
    return pl.pallas_call(
        gram_kernel,
        grid=(cap,),
        in_specs=[half, half, stat, stat],
        out_specs=[stat, stat],
        out_shape=[jax.ShapeDtypeStruct(left.shape, BF16)] * 2,
        compiler_params=params(),
        cost_estimate=cost(4 * cap * block**3, 10 * cap * block * block),
        name="grams",
    )(upper, lower, left, right)


def total(*terms):
    return functools.reduce(jnp.add, [t.astype(F32) for t in terms]).astype(BF16)


def added(own, at, term):
    n = term.shape[0]
    return lax.dynamic_update_slice(own, total(own[at : at + n], term), (at,) + (0,) * (own.ndim - 1))


def fold_kernel(own, first, last, here, one, three, two_low, two_high):
    def unit(t):
        return total(own[t], first[t], last[t])

    half = two_low.shape[0]
    two = unit(2)
    two_low[...] = two[:half]
    two_high[...] = two[half:]
    one[...] = unit(1)
    three[...] = unit(3)
    here[...] = unit(0)


def fold(own, first, last):
    _, half, block = own.shape
    whole, part = jax.ShapeDtypeStruct((half, block), BF16), jax.ShapeDtypeStruct((half // 2, block), BF16)
    return pl.pallas_call(
        fold_kernel,
        out_shape=[whole, whole, whole, part, part],
        compiler_params=params(),
        cost_estimate=cost(0, 8 * half * block),
        name="fold",
    )(own, first, last)


def finish_kernel(own, first, last, out):
    out[...] = total(own[...], first[...], last[...])


def finish(own, first, last):
    return pl.pallas_call(
        finish_kernel,
        out_shape=jax.ShapeDtypeStruct(own.shape, BF16),
        compiler_params=params(),
        cost_estimate=cost(0, 8 * own.size),
        name="finish",
    )(own, first, last)


def shards(inputs, output_grads, owner_map, left_stats, right_stats, left_roots, right_roots):
    block = left_stats.shape[-1]
    cap = left_stats.shape[2]
    opt_count = lax.axis_size("opt")
    shard = lax.axis_index("opt")
    home = lax.axis_index("dp")
    chooser = (shard * 4 // opt_count == 3).astype(jnp.int32)
    place = jnp.stack([chooser, home // SIDE, home % SIDE])

    owners = owner_map[0]
    places = jnp.arange(opt_count, dtype=jnp.int32)
    same = (owners[None, :] == owners[:, None]) & (places[None, :] < places[:, None])
    slots = owners * cap + jnp.sum(same.astype(jnp.int32), axis=1)
    slot_ids = jnp.arange(opt_count * cap, dtype=jnp.int32)
    holders = slots[None, :] == slot_ids[:, None]
    homes = jnp.sum(jnp.where(holders, places[None, :] + 1, 0), axis=1) - 1

    def chunks(count, first, per_out):
        return partials(inputs, output_grads, place, count, first, per_out, block)

    a2l, a2h, b2l, b2h = chunks(2, 2, 2)
    a1, a3, b1, b3 = chunks(4, 1, 4)
    a0, b0 = chunks(2, 0, 4)

    right, left = x_ring(1), x_ring(-1)
    down, up = y_ring(1), y_ring(-1)

    def send(value, ring):
        return lax.ppermute(value, "dp", ring)

    packed = pack_roots(left_roots[0, 0], right_roots[0, 0], opt_count)

    a_r1, a_l1 = send(a2l, right), send(a2h, left)
    b_r1, b_l1 = send(b2l, down), send(b2h, up)

    spread = lax.all_to_all(packed, "opt", 0, 0, tiled=True)

    a_r2, a_l2 = send(added(a1, 0, a_r1), right), send(added(a3, 2, a_l1), left)
    b_r2, b_l2 = send(added(b1, 0, b_r1), down), send(added(b3, 2, b_l1), up)

    chosen = pick_roots(slots, spread, cap)
    gathered = lax.all_to_all(chosen, "opt", 0, 0, tiled=True)
    rank = lax.dynamic_slice(slots, (shard,), (1,)) % cap
    roots = unpack_roots(rank, gathered, block)

    a0, b0, chosen = lax.optimization_barrier((a0, b0, chosen))
    a0, a1, a3, a2l, a2h = fold(a0, a_r2, a_l2)
    b0, b1, b3, b2l, b2h = fold(b0, b_r2, b_l2)

    part = block // 4
    a_r1, a_l1 = send(a2l, down), send(a2h, up)
    b_r1, b_l1 = send(b2l, right), send(b2h, left)
    a_r2, a_l2 = send(added(a1, 0, a_r1), down), send(added(a3, part, a_l1), up)
    b_r2, b_l2 = send(added(b1, 0, b_r1), right), send(added(b3, part, b_l1), left)
    halves = [finish(b0, b_r2, b_l2), finish(a0, a_r2, a_l2)]
    halves[1], roots = lax.optimization_barrier((halves[1], roots))

    owned = []
    for half in halves:
        rows = half.shape[0] // opt_count
        spread = lax.all_to_all(half.reshape(opt_count, rows, block), "opt", 0, 0, tiled=True)
        picked = pick(homes, spread).reshape(opt_count, cap, rows, block)
        owned.append(lax.all_to_all(picked, "opt", 0, 0, tiled=True))
    update = precondition(roots, halves[1], halves[0])
    left_updated, right_updated = grams(owned[1], owned[0], left_stats[0, 0], right_stats[0, 0])
    return update[None, None], left_updated[None, None], right_updated[None, None]


def solution(mesh):
    return jax.shard_map(
        shards,
        mesh=mesh,
        in_specs=(
            P(None, "dp", None),
            P("dp", "opt"),
            P("dp", None),
            P("dp", "opt", None, None, None),
            P("dp", "opt", None, None, None),
            P("dp", "opt", None, None, None),
            P("dp", "opt", None, None, None),
        ),
        out_specs=(
            P("opt", "dp", None, None),
            P("dp", "opt", None, None, None),
            P("dp", "opt", None, None, None),
        ),
        check_vma=False,
    )
```

```python
import functools

import jax
import jax.numpy as jnp
from jax import lax
from jax.experimental import pallas as pl
from jax.experimental.pallas import tpu as pltpu
from jax.sharding import PartitionSpec as P

DECAY_RATE = 0.95
SIDE = 4
OFF = [(i, j) for i in range(4) for j in range(i + 1, 4)]
VMEM_BYTES = 20 * 1024 * 1024
EXTRA = 16
F32 = jnp.float32
BF16 = jnp.bfloat16


def params(limit=VMEM_BYTES):
    return pltpu.CompilerParams(vmem_limit_bytes=limit)


def cost(flops, moved):
    return pl.CostEstimate(flops=int(flops), bytes_accessed=int(moved), transcendentals=0)


def x_ring(step):
    return [(y * SIDE + x, y * SIDE + (x + step) % SIDE) for y in range(SIDE) for x in range(SIDE)]


def y_ring(step):
    return [(y * SIDE + x, ((y + step) % SIDE) * SIDE + x) for y in range(SIDE) for x in range(SIDE)]


def dot(a, b, over_a, over_b):
    return lax.dot_general(a, b, (((over_a,), (over_b,)), ((), ())), preferred_element_type=F32)


def partial_kernel(place, source, target, *refs):
    count = (len(refs) - 4) // 2
    results, outs, (rows, cols, sems, out_sems) = refs[:count], refs[count : 2 * count], refs[2 * count :]
    a2l, a2h, b2l, b2h, a1l, a1h, b1l, b1h, a3l, a3h, b3l, b3h, a0, b0 = outs
    block = cols.shape[1] // 2
    half = block // 2
    chooser, y, x = place[0], place[1], place[2]

    def copy_rows(i):
        side = lax.div(lax.rem(x + 2, SIDE), 2)
        side = side if i < SIDE else 1 - side
        at = pl.ds(pl.multiple_of((2 * lax.rem(y + i, SIDE) + side) * block, block), block)
        return pltpu.make_async_copy(source.at[chooser, :, at], rows.at[:, at], sems.at[i])

    copies = [copy_rows(i) for i in range(2 * SIDE)]
    copies.append(pltpu.make_async_copy(target, cols, sems.at[2 * SIDE]))
    for i in (2 * SIDE, *range(2 * SIDE)):
        copies[i].start()

    def unit(k_y, k_x, lower):
        row = pl.multiple_of((2 * k_y + lax.div(k_x, 2)) * block + lower * half, half)
        col = pl.multiple_of(lax.rem(k_x, 2) * block, block)
        return dot(rows[:, pl.ds(row, half)], cols[:, pl.ds(col, block)], 0, 0).astype(BF16)

    leaving = []

    def fill(parts, units):
        for t, value in enumerate(units):
            part, at = divmod(t, parts[0].shape[0])
            parts[part][at] = value()
            if at == parts[0].shape[0] - 1:
                o = [i for i, out in enumerate(outs) if out is parts[part]][0]
                leaving.append(pltpu.make_async_copy(outs[o], results[o], out_sems.at[o]))
                leaving[-1].start()

    def chunk_a(r, *parts):
        fill(parts, [functools.partial(unit, lax.rem(y + t, SIDE), lax.rem(x + r, SIDE), 0) for t in range(SIDE)])

    def chunk_b(r, *parts):
        fill(parts, [functools.partial(unit, lax.rem(y + r, SIDE), lax.rem(x + t, SIDE), 1) for t in range(SIDE)])

    for i in (2 * SIDE, *range(SIDE)):
        copies[i].wait()
    chunk_a(2, a2l, a2h)
    for i in range(SIDE, 2 * SIDE):
        copies[i].wait()
    chunk_b(2, b2l, b2h)
    chunk_a(1, a1l, a1h)
    chunk_b(1, b1l, b1h)
    chunk_a(3, a3l, a3h)
    chunk_b(3, b3l, b3h)
    chunk_a(0, a0)
    chunk_b(0, b0)
    for copy in leaving:
        copy.wait()


def partials(inputs, output_grads, place, block):
    tok, feats = inputs.shape[1:]
    half = block // 2
    sizes = [2] * 12 + [SIDE] * 2
    units = sum(sizes)
    hbm = pl.BlockSpec(memory_space=pltpu.HBM)
    return pl.pallas_call(
        partial_kernel,
        in_specs=[pl.BlockSpec(memory_space=pltpu.SMEM), hbm, hbm],
        out_specs=[hbm] * len(sizes),
        out_shape=[pltpu.HBM((n, half, block), BF16) for n in sizes],
        scratch_shapes=[pltpu.VMEM((n, half, block), BF16) for n in sizes]
        + [
            pltpu.VMEM((tok, feats), BF16),
            pltpu.VMEM(output_grads.shape, BF16),
            pltpu.SemaphoreType.DMA((2 * SIDE + 1,)),
            pltpu.SemaphoreType.DMA((len(sizes),)),
        ],
        compiler_params=params(),
        cost_estimate=cost(
            2 * units * tok * half * block,
            2 * (tok * feats + output_grads.size + units * half * block),
        ),
        name="partials",
    )(
        place,
        pltpu.with_memory_space_constraint(inputs, pltpu.HBM),
        pltpu.with_memory_space_constraint(output_grads, pltpu.HBM),
    )


def grid_masks(n):
    rows = lax.broadcasted_iota(jnp.int32, (n, n), 0)
    cols = lax.broadcasted_iota(jnp.int32, (n, n), 1)
    return rows, cols


def pack_kernel(left, right, out):
    q = left.shape[-1] // 4
    parts = out.shape[0]
    per = parts // 8
    step = q // per
    rows, cols = grid_masks(q)

    def put(slot, piece, value):
        for h in range(per):
            out[piece * per + h, slot * step : (slot + 1) * step] = value[h * step : (h + 1) * step]

    lines = []
    for c in range(left.shape[0]):
        for m, ref in enumerate((left, right)):

            def quarter(i, j, ref=ref, c=c):
                return ref[c, i * q : (i + 1) * q, j * q : (j + 1) * q]

            for n, (i, j) in enumerate(OFF):
                put(2 * c + m, n, quarter(i, j))
            for h in range(2):
                upper, lower = quarter(2 * h, 2 * h), quarter(2 * h + 1, 2 * h + 1)
                put(2 * c + m, len(OFF) + h, jnp.where(rows <= cols, upper, lower))
                lines.append(jnp.sum(jnp.where(rows == cols, lower.astype(F32), 0.0), axis=0, keepdims=True))
    lines.append(jnp.zeros((EXTRA - len(lines), q), F32))
    extra = jnp.concatenate(lines, axis=0).astype(BF16)
    for j in range(parts):
        out[j, 2 * left.shape[0] * step :] = extra


def pack_roots(left, right, parts):
    cap, block = left.shape[0], left.shape[-1]
    q = block // 4
    shape = (parts, 2 * cap * (8 * q // parts) + EXTRA, q)
    return pl.pallas_call(
        pack_kernel,
        out_shape=jax.ShapeDtypeStruct(shape, BF16),
        compiler_params=params(),
        cost_estimate=cost(0, 3 * 2 * left.size),
        name="pack_roots",
    )(left, right)


def pick_roots_kernel(slots, src, out):
    body = out.shape[1] - EXTRA
    cap = (src.shape[1] - EXTRA) // body
    for i in range(out.shape[0]):
        owner, rank = lax.div(slots[i], cap), lax.rem(slots[i], cap)
        out[i, :body] = src[owner, pl.ds(pl.multiple_of(rank * body, body), body)]
        out[i, body:] = src[owner, cap * body :]


def pick_roots(slots, src, cap):
    rows = (src.shape[1] - EXTRA) // cap + EXTRA
    return pl.pallas_call(
        pick_roots_kernel,
        in_specs=[pl.BlockSpec(memory_space=pltpu.SMEM), pl.BlockSpec(memory_space=pltpu.VMEM)],
        out_specs=pl.BlockSpec(memory_space=pltpu.VMEM),
        out_shape=jax.ShapeDtypeStruct((slots.shape[0], rows, src.shape[2]), src.dtype),
        compiler_params=params(),
        cost_estimate=cost(0, 4 * src.size),
        name="pick_roots",
    )(slots, src)


def pick_kernel(index, src, out):
    for i in range(out.shape[0]):
        at = index[i]

        @pl.when(at >= 0)
        def _(i=i, at=at):
            out[i] = src[jnp.maximum(at, 0)]

        @pl.when(at < 0)
        def _(i=i):
            out[i] = jnp.zeros(out.shape[1:], out.dtype)


def pick(index, src):
    shape = (index.shape[0],) + src.shape[1:]
    return pl.pallas_call(
        pick_kernel,
        in_specs=[pl.BlockSpec(memory_space=pltpu.SMEM), pl.BlockSpec(memory_space=pltpu.VMEM)],
        out_specs=pl.BlockSpec(memory_space=pltpu.VMEM),
        out_shape=jax.ShapeDtypeStruct(shape, src.dtype),
        compiler_params=params(),
        cost_estimate=cost(0, 4 * src.size),
        name="pick",
    )(index, src)


def unpack_kernel(ranks, packed, out):
    q = out.shape[-1] // 4
    per = packed.shape[0] // 8
    step = q // per
    rows, cols = grid_masks(q)
    rank = ranks[0]
    lines = packed[0, 2 * step :].astype(F32)
    for m in range(2):

        def piece(n, m=m):
            return jnp.concatenate([packed[n * per + h, m * step : (m + 1) * step] for h in range(per)], axis=0)

        def put(i, j, value, m=m):
            out[m, i * q : (i + 1) * q, j * q : (j + 1) * q] = value

        for n, (i, j) in enumerate(OFF):
            value = piece(n)
            put(i, j, value)
            put(j, i, value.T)
        for h in range(2):
            value = piece(len(OFF) + h)
            turned = value.T
            put(2 * h, 2 * h, jnp.where(rows <= cols, value, turned))
            own = lines[2 * m + h : 2 * m + h + 1, :]
            for c in range(1, (EXTRA // 4)):
                at = 4 * c + 2 * m + h
                own = jnp.where(rank == c, lines[at : at + 1, :], own)
            own = jnp.broadcast_to(own, (q, q)).astype(BF16)
            lower = jnp.where(rows > cols, value, turned)
            put(2 * h + 1, 2 * h + 1, jnp.where(rows == cols, own, lower))


def unpack_roots(rank, packed, block):
    return pl.pallas_call(
        unpack_kernel,
        in_specs=[pl.BlockSpec(memory_space=pltpu.SMEM), pl.BlockSpec(memory_space=pltpu.VMEM)],
        out_specs=pl.BlockSpec(memory_space=pltpu.VMEM),
        out_shape=jax.ShapeDtypeStruct((2, block, block), BF16),
        compiler_params=params(),
        cost_estimate=cost(0, 8 * block * block),
        name="unpack_roots",
    )(rank, packed)


def update_kernel(roots, grad, out):
    twisted = dot(grad[...], roots[1], 1, 0).astype(BF16)
    out[...] = dot(roots[0], twisted, 1, 0).astype(BF16)


def precondition(roots, grad):
    block = grad.shape[-1]
    return pl.pallas_call(
        update_kernel,
        out_shape=jax.ShapeDtypeStruct(grad.shape, BF16),
        compiler_params=params(),
        cost_estimate=cost(4 * block**3, 8 * block * block),
        name="precondition",
    )(roots, grad)


def gram_kernel(grads, left, right, left_out, right_out):
    block = left.shape[-1]
    grad = grads[...].reshape(block, block)
    gram = dot(grad, grad, 1, 1)
    left_out[...] = (left[...].astype(F32) * DECAY_RATE + gram / block).astype(BF16)
    gram = dot(grad, grad, 0, 0)
    right_out[...] = (right[...].astype(F32) * DECAY_RATE + gram / block).astype(BF16)


def grams(grads, left, right):
    parts, cap, rows, block = grads.shape
    stat = pl.BlockSpec((None, block, block), lambda c: (c, 0, 0))
    return pl.pallas_call(
        gram_kernel,
        grid=(cap,),
        in_specs=[pl.BlockSpec((parts, None, rows, block), lambda c: (0, c, 0, 0)), stat, stat],
        out_specs=[stat, stat],
        out_shape=[jax.ShapeDtypeStruct(left.shape, BF16)] * 2,
        compiler_params=params(),
        cost_estimate=cost(4 * cap * block**3, 10 * cap * block * block),
        name="grams",
    )(grads, left, right)


def total(*terms):
    return functools.reduce(jnp.add, [t.astype(F32) for t in terms]).astype(BF16)


def joined(first, last):
    return jnp.concatenate([first, last], axis=0)


def fold_kernel(own, first, last, *outs):
    for t, out in enumerate(outs):
        out[...] = total(own[t], first[t], last[t])


def fold(own, first, last):
    _, half, block = own.shape
    return pl.pallas_call(
        fold_kernel,
        out_shape=[jax.ShapeDtypeStruct((half, block), BF16)] * SIDE,
        compiler_params=params(),
        cost_estimate=cost(0, 8 * half * block),
        name="fold",
    )(own, first, last)


def finish_kernel(*refs):
    terms, out = refs[:-1], refs[-1]
    half = out.shape[0] // 2
    out[:half] = total(*[t[...] for t in terms[:SIDE]])
    out[half:] = total(*[t[...] for t in terms[SIDE:]])


def finish(*terms):
    half, block = terms[0].shape
    return pl.pallas_call(
        finish_kernel,
        out_shape=jax.ShapeDtypeStruct((2 * half, block), BF16),
        compiler_params=params(),
        cost_estimate=cost(0, 20 * half * block),
        name="finish",
    )(*terms)


def shards(inputs, output_grads, owner_map, left_stats, right_stats, left_roots, right_roots):
    block = left_stats.shape[-1]
    cap = left_stats.shape[2]
    opt_count = lax.axis_size("opt")
    shard = lax.axis_index("opt")
    home = lax.axis_index("dp")
    chooser = (shard * 4 // opt_count == 3).astype(jnp.int32)
    place = jnp.stack([chooser, home // SIDE, home % SIDE])

    owners = owner_map[0]
    places = jnp.arange(opt_count, dtype=jnp.int32)
    same = (owners[None, :] == owners[:, None]) & (places[None, :] < places[:, None])
    slots = owners * cap + jnp.sum(same.astype(jnp.int32), axis=1)
    slot_ids = jnp.arange(opt_count * cap, dtype=jnp.int32)
    holders = slots[None, :] == slot_ids[:, None]
    homes = jnp.sum(jnp.where(holders, places[None, :] + 1, 0), axis=1) - 1

    a2l, a2h, b2l, b2h, a1l, a1h, b1l, b1h, a3l, a3h, b3l, b3h, a0, b0 = partials(inputs, output_grads, place, block)

    right, left = x_ring(1), x_ring(-1)
    down, up = y_ring(1), y_ring(-1)

    def send(value, ring):
        return lax.ppermute(value, "dp", ring)

    packed = pack_roots(left_roots[0, 0], right_roots[0, 0], opt_count)

    a_r1, a_l1 = send(a2l, right), send(a2h, left)
    b_r1, b_l1 = send(b2l, down), send(b2h, up)

    spread = lax.all_to_all(packed, "opt", 0, 0, tiled=True)

    a_r2, a_l2 = send(joined(total(a1l, a_r1), a1h), right), send(joined(a3l, total(a3h, a_l1)), left)
    b_r2, b_l2 = send(joined(total(b1l, b_r1), b1h), down), send(joined(b3l, total(b3h, b_l1)), up)

    chosen = pick_roots(slots, spread, cap)
    a0, b0, chosen = lax.optimization_barrier((a0, b0, chosen))
    a_units, b_units = fold(a0, a_r2, a_l2), fold(b0, b_r2, b_l2)

    b_terms = [b_units[0]] + [send(b_units[t], x_ring(t)) for t in (2, 1, 3)]
    a_terms = [a_units[0]] + [send(a_units[t], y_ring(t)) for t in (2, 1, 3)]

    gathered = lax.all_to_all(chosen, "opt", 0, 0, tiled=True)
    rank = lax.dynamic_slice(slots, (shard,), (1,)) % cap
    roots = unpack_roots(rank, gathered, block)

    grad = finish(*a_terms, *b_terms)
    grad, roots = lax.optimization_barrier((grad, roots))

    rows = block // opt_count
    spread = lax.all_to_all(grad.reshape(opt_count, rows, block), "opt", 0, 0, tiled=True)
    picked = pick(homes, spread).reshape(opt_count, cap, rows, block)
    owned = lax.all_to_all(picked, "opt", 0, 0, tiled=True)
    update = precondition(roots, grad)
    left_updated, right_updated = grams(owned, left_stats[0, 0], right_stats[0, 0])
    return update[None, None], left_updated[None, None], right_updated[None, None]


def solution(mesh):
    return jax.shard_map(
        shards,
        mesh=mesh,
        in_specs=(
            P(None, "dp", None),
            P("dp", "opt"),
            P("dp", None),
            P("dp", "opt", None, None, None),
            P("dp", "opt", None, None, None),
            P("dp", "opt", None, None, None),
            P("dp", "opt", None, None, None),
        ),
        out_specs=(
            P("opt", "dp", None, None),
            P("dp", "opt", None, None, None),
            P("dp", "opt", None, None, None),
        ),
        check_vma=False,
    )
```

```python
import functools

import jax
import jax.numpy as jnp
from jax import lax
from jax.experimental import pallas as pl
from jax.experimental.pallas import tpu as pltpu
from jax.sharding import PartitionSpec as P

DECAY_RATE = 0.95
SIDE = 4
OFF = [(i, j) for i in range(4) for j in range(i + 1, 4)]
VMEM_BYTES = 20 * 1024 * 1024
EXTRA = 16
F32 = jnp.float32
BF16 = jnp.bfloat16


def params(limit=VMEM_BYTES):
    return pltpu.CompilerParams(vmem_limit_bytes=limit)


def cost(flops, moved):
    return pl.CostEstimate(flops=int(flops), bytes_accessed=int(moved), transcendentals=0)


def x_ring(step):
    return [(y * SIDE + x, y * SIDE + (x + step) % SIDE) for y in range(SIDE) for x in range(SIDE)]


def y_ring(step):
    return [(y * SIDE + x, ((y + step) % SIDE) * SIDE + x) for y in range(SIDE) for x in range(SIDE)]


def dot(a, b, over_a, over_b):
    return lax.dot_general(a, b, (((over_a,), (over_b,)), ((), ())), preferred_element_type=F32)


def partial_kernel(place, source, target, *refs):
    count = (len(refs) - 4) // 2
    results, outs, (rows, cols, sems, out_sems) = refs[:count], refs[count : 2 * count], refs[2 * count :]
    a2l, a2h, b2l, b2h, a1l, a1h, b1l, b1h, a3l, a3h, b3l, b3h, a0, b0 = outs
    block = cols.shape[1] // 2
    half = block // 2
    chooser, y, x = place[0], place[1], place[2]

    def copy_rows(i):
        side = lax.div(lax.rem(x + 2, SIDE), 2)
        side = side if i < SIDE else 1 - side
        at = pl.ds(pl.multiple_of((2 * lax.rem(y + i, SIDE) + side) * block, block), block)
        return pltpu.make_async_copy(source.at[chooser, :, at], rows.at[:, at], sems.at[i])

    copies = [copy_rows(i) for i in range(2 * SIDE)]
    copies.append(pltpu.make_async_copy(target, cols, sems.at[2 * SIDE]))
    for i in (2 * SIDE, *range(2 * SIDE)):
        copies[i].start()

    def unit(k_y, k_x, lower):
        row = pl.multiple_of((2 * k_y + lax.div(k_x, 2)) * block + lower * half, half)
        col = pl.multiple_of(lax.rem(k_x, 2) * block, block)
        return dot(rows[:, pl.ds(row, half)], cols[:, pl.ds(col, block)], 0, 0).astype(BF16)

    leaving = []

    def fill(parts, units):
        for t, value in enumerate(units):
            part, at = divmod(t, parts[0].shape[0])
            parts[part][at] = value()
            if at == parts[0].shape[0] - 1:
                o = [i for i, out in enumerate(outs) if out is parts[part]][0]
                leaving.append(pltpu.make_async_copy(outs[o], results[o], out_sems.at[o]))
                leaving[-1].start()

    def chunk_a(r, *parts):
        fill(parts, [functools.partial(unit, lax.rem(y + t, SIDE), lax.rem(x + r, SIDE), 0) for t in range(SIDE)])

    def chunk_b(r, *parts):
        fill(parts, [functools.partial(unit, lax.rem(y + r, SIDE), lax.rem(x + t, SIDE), 1) for t in range(SIDE)])

    for i in (2 * SIDE, *range(SIDE)):
        copies[i].wait()
    chunk_a(2, a2l, a2h)
    for i in range(SIDE, 2 * SIDE):
        copies[i].wait()
    chunk_b(2, b2l, b2h)
    chunk_a(1, a1l, a1h)
    chunk_b(1, b1l, b1h)
    chunk_a(3, a3l, a3h)
    chunk_b(3, b3l, b3h)
    chunk_a(0, a0)
    chunk_b(0, b0)
    for copy in leaving:
        copy.wait()


def partials(inputs, output_grads, place, block):
    tok, feats = inputs.shape[1:]
    half = block // 2
    sizes = [2] * 12 + [SIDE] * 2
    units = sum(sizes)
    hbm = pl.BlockSpec(memory_space=pltpu.HBM)
    return pl.pallas_call(
        partial_kernel,
        in_specs=[pl.BlockSpec(memory_space=pltpu.SMEM), hbm, hbm],
        out_specs=[hbm] * len(sizes),
        out_shape=[pltpu.HBM((n, half, block), BF16) for n in sizes],
        scratch_shapes=[pltpu.VMEM((n, half, block), BF16) for n in sizes]
        + [
            pltpu.VMEM((tok, feats), BF16),
            pltpu.VMEM(output_grads.shape, BF16),
            pltpu.SemaphoreType.DMA((2 * SIDE + 1,)),
            pltpu.SemaphoreType.DMA((len(sizes),)),
        ],
        compiler_params=params(),
        cost_estimate=cost(
            2 * units * tok * half * block,
            2 * (tok * feats + output_grads.size + units * half * block),
        ),
        name="partials",
    )(
        place,
        pltpu.with_memory_space_constraint(inputs, pltpu.HBM),
        pltpu.with_memory_space_constraint(output_grads, pltpu.HBM),
    )


def grid_masks(n):
    rows = lax.broadcasted_iota(jnp.int32, (n, n), 0)
    cols = lax.broadcasted_iota(jnp.int32, (n, n), 1)
    return rows, cols


def pack_kernel(left, right, out):
    q = left.shape[-1] // 4
    parts = out.shape[0]
    per = parts // 8
    step = q // per
    rows, cols = grid_masks(q)

    def put(slot, piece, value):
        for h in range(per):
            out[piece * per + h, slot * step : (slot + 1) * step] = value[h * step : (h + 1) * step]

    lines = []
    for c in range(left.shape[0]):
        for m, ref in enumerate((left, right)):

            def quarter(i, j, ref=ref, c=c):
                return ref[c, i * q : (i + 1) * q, j * q : (j + 1) * q]

            for n, (i, j) in enumerate(OFF):
                put(2 * c + m, n, quarter(i, j))
            for h in range(2):
                upper, lower = quarter(2 * h, 2 * h), quarter(2 * h + 1, 2 * h + 1)
                put(2 * c + m, len(OFF) + h, jnp.where(rows <= cols, upper, lower))
                lines.append(jnp.sum(jnp.where(rows == cols, lower.astype(F32), 0.0), axis=0, keepdims=True))
    lines.append(jnp.zeros((EXTRA - len(lines), q), F32))
    extra = jnp.concatenate(lines, axis=0).astype(BF16)
    for j in range(parts):
        out[j, 2 * left.shape[0] * step :] = extra


def pack_roots(left, right, parts):
    cap, block = left.shape[0], left.shape[-1]
    q = block // 4
    shape = (parts, 2 * cap * (8 * q // parts) + EXTRA, q)
    return pl.pallas_call(
        pack_kernel,
        out_shape=jax.ShapeDtypeStruct(shape, BF16),
        compiler_params=params(),
        cost_estimate=cost(0, 3 * 2 * left.size),
        name="pack_roots",
    )(left, right)


def pick_roots_kernel(slots, src, out):
    body = out.shape[1] - EXTRA
    cap = (src.shape[1] - EXTRA) // body
    for i in range(out.shape[0]):
        owner, rank = lax.div(slots[i], cap), lax.rem(slots[i], cap)
        out[i, :body] = src[owner, pl.ds(pl.multiple_of(rank * body, body), body)]
        out[i, body:] = src[owner, cap * body :]


def pick_roots(slots, src, cap):
    rows = (src.shape[1] - EXTRA) // cap + EXTRA
    return pl.pallas_call(
        pick_roots_kernel,
        in_specs=[pl.BlockSpec(memory_space=pltpu.SMEM), pl.BlockSpec(memory_space=pltpu.VMEM)],
        out_specs=pl.BlockSpec(memory_space=pltpu.VMEM),
        out_shape=jax.ShapeDtypeStruct((slots.shape[0], rows, src.shape[2]), src.dtype),
        compiler_params=params(),
        cost_estimate=cost(0, 4 * src.size),
        name="pick_roots",
    )(slots, src)


def unpack_kernel(ranks, packed, out):
    q = out.shape[-1] // 4
    per = packed.shape[0] // 8
    step = q // per
    rows, cols = grid_masks(q)
    rank = ranks[0]
    lines = packed[0, 2 * step :].astype(F32)
    for m in range(2):

        def piece(n, m=m):
            return jnp.concatenate([packed[n * per + h, m * step : (m + 1) * step] for h in range(per)], axis=0)

        def put(i, j, value, m=m):
            out[m, i * q : (i + 1) * q, j * q : (j + 1) * q] = value

        for n, (i, j) in enumerate(OFF):
            value = piece(n)
            put(i, j, value)
            put(j, i, value.T)
        for h in range(2):
            value = piece(len(OFF) + h)
            turned = value.T
            put(2 * h, 2 * h, jnp.where(rows <= cols, value, turned))
            own = lines[2 * m + h : 2 * m + h + 1, :]
            for c in range(1, (EXTRA // 4)):
                at = 4 * c + 2 * m + h
                own = jnp.where(rank == c, lines[at : at + 1, :], own)
            own = jnp.broadcast_to(own, (q, q)).astype(BF16)
            lower = jnp.where(rows > cols, value, turned)
            put(2 * h + 1, 2 * h + 1, jnp.where(rows == cols, own, lower))


def unpack_roots(rank, packed, block):
    return pl.pallas_call(
        unpack_kernel,
        in_specs=[pl.BlockSpec(memory_space=pltpu.SMEM), pl.BlockSpec(memory_space=pltpu.VMEM)],
        out_specs=pl.BlockSpec(memory_space=pltpu.VMEM),
        out_shape=jax.ShapeDtypeStruct((2, block, block), BF16),
        compiler_params=params(),
        cost_estimate=cost(0, 8 * block * block),
        name="unpack_roots",
    )(rank, packed)


def update_kernel(roots, upper, lower, out):
    half = upper.shape[0]
    twisted = [dot(part[...], roots[1], 1, 0).astype(BF16) for part in (upper, lower)]
    out[...] = (dot(roots[0, :, :half], twisted[0], 1, 0) + dot(roots[0, :, half:], twisted[1], 1, 0)).astype(BF16)


def precondition(roots, upper, lower):
    block = upper.shape[-1]
    return pl.pallas_call(
        update_kernel,
        out_shape=jax.ShapeDtypeStruct((block, block), BF16),
        compiler_params=params(),
        cost_estimate=cost(4 * block**3, 8 * block * block),
        name="precondition",
    )(roots, upper, lower)


def gram_kernel(homes, upper, lower, left, right, left_out, right_out):
    block = left.shape[-1]
    half = block // 2
    present = (homes[pl.program_id(0)] >= 0).astype(F32) / block
    parts = [upper[...], lower[...]]
    for i in range(2):
        for j in range(2):
            at = slice(i * half, (i + 1) * half), slice(j * half, (j + 1) * half)
            gram = dot(parts[i], parts[j], 1, 1)
            left_out[at] = (left[at].astype(F32) * DECAY_RATE + gram * present).astype(BF16)
    gram = dot(parts[0], parts[0], 0, 0) + dot(parts[1], parts[1], 0, 0)
    right_out[...] = (right[...].astype(F32) * DECAY_RATE + gram * present).astype(BF16)


def grams(homes, upper, lower, left, right):
    cap, block, _ = left.shape
    stat = pl.BlockSpec((None, block, block), lambda c, h: (c, 0, 0))
    part = pl.BlockSpec((None, block // 2, block), lambda c, h: (jnp.maximum(h[c], 0), 0, 0))
    return pl.pallas_call(
        gram_kernel,
        grid_spec=pltpu.PrefetchScalarGridSpec(
            num_scalar_prefetch=1,
            grid=(cap,),
            in_specs=[part, part, stat, stat],
            out_specs=[stat, stat],
        ),
        out_shape=[jax.ShapeDtypeStruct(left.shape, BF16)] * 2,
        compiler_params=params(),
        cost_estimate=cost(4 * cap * block**3, 10 * cap * block * block),
        name="grams",
    )(
        homes,
        pltpu.with_memory_space_constraint(upper, pltpu.HBM),
        pltpu.with_memory_space_constraint(lower, pltpu.HBM),
        left,
        right,
    )


def total(*terms):
    return functools.reduce(jnp.add, [t.astype(F32) for t in terms]).astype(BF16)


def joined(first, last):
    return jnp.concatenate([first, last], axis=0)


def fold_kernel(own, first, last, *outs):
    for t, out in enumerate(outs):
        out[...] = total(own[t], first[t], last[t])


def fold(own, first, last):
    _, half, block = own.shape
    return pl.pallas_call(
        fold_kernel,
        out_shape=[jax.ShapeDtypeStruct((half, block), BF16)] * SIDE,
        compiler_params=params(),
        cost_estimate=cost(0, 8 * half * block),
        name="fold",
    )(own, first, last)


def finish_kernel(*refs):
    refs[-1][...] = total(*[t[...] for t in refs[:-1]])


def finish(*terms):
    return pl.pallas_call(
        finish_kernel,
        out_shape=jax.ShapeDtypeStruct(terms[0].shape, BF16),
        compiler_params=params(),
        cost_estimate=cost(0, 2 * (len(terms) + 1) * terms[0].size),
        name="finish",
    )(*terms)


def shards(inputs, output_grads, owner_map, left_stats, right_stats, left_roots, right_roots):
    block = left_stats.shape[-1]
    cap = left_stats.shape[2]
    opt_count = lax.axis_size("opt")
    shard = lax.axis_index("opt")
    home = lax.axis_index("dp")
    chooser = (shard * 4 // opt_count == 3).astype(jnp.int32)
    place = jnp.stack([chooser, home // SIDE, home % SIDE])

    owners = owner_map[0]
    places = jnp.arange(opt_count, dtype=jnp.int32)
    same = (owners[None, :] == owners[:, None]) & (places[None, :] < places[:, None])
    slots = owners * cap + jnp.sum(same.astype(jnp.int32), axis=1)
    slot_ids = shard * cap + jnp.arange(cap, dtype=jnp.int32)
    holders = slots[None, :] == slot_ids[:, None]
    homes = jnp.sum(jnp.where(holders, places[None, :] + 1, 0), axis=1) - 1

    a2l, a2h, b2l, b2h, a1l, a1h, b1l, b1h, a3l, a3h, b3l, b3h, a0, b0 = partials(inputs, output_grads, place, block)

    right, left = x_ring(1), x_ring(-1)
    down, up = y_ring(1), y_ring(-1)

    def send(value, ring):
        return lax.ppermute(value, "dp", ring)

    packed = pack_roots(left_roots[0, 0], right_roots[0, 0], opt_count)

    a_r1, a_l1 = send(a2l, right), send(a2h, left)
    b_r1, b_l1 = send(b2l, down), send(b2h, up)

    spread = lax.all_to_all(packed, "opt", 0, 0, tiled=True)
    a_r1, a_l1, b_r1, b_l1 = lax.optimization_barrier((a_r1, a_l1, b_r1, b_l1))

    a_r2, a_l2 = send(joined(total(a1l, a_r1), a1h), right), send(joined(a3l, total(a3h, a_l1)), left)
    b_r2, b_l2 = send(joined(total(b1l, b_r1), b1h), down), send(joined(b3l, total(b3h, b_l1)), up)

    chosen = pick_roots(slots, spread, cap)
    a_r2, a_l2, b_r2, b_l2, chosen = lax.optimization_barrier((a_r2, a_l2, b_r2, b_l2, chosen))
    a_units, b_units = fold(a0, a_r2, a_l2), fold(b0, b_r2, b_l2)

    b_terms = [b_units[0]] + [send(b_units[t], x_ring(t)) for t in (2, 1, 3)]
    a_terms = [a_units[0]] + [send(a_units[t], y_ring(t)) for t in (2, 1, 3)]

    gathered = lax.all_to_all(chosen, "opt", 0, 0, tiled=True)
    rank = lax.dynamic_slice(slots, (shard,), (1,)) % cap
    b_terms, gathered = lax.optimization_barrier((b_terms, gathered))
    lower = finish(*b_terms)
    all_lower = lax.all_gather(lower, "opt", axis=0)
    upper = finish(*a_terms)
    all_upper = lax.all_gather(upper, "opt", axis=0)
    roots = unpack_roots(rank, gathered, block)
    update = precondition(roots, upper, lower)
    left_updated, right_updated = grams(homes, all_upper, all_lower, left_stats[0, 0], right_stats[0, 0])
    return update[None, None], left_updated[None, None], right_updated[None, None]


def solution(mesh):
    return jax.shard_map(
        shards,
        mesh=mesh,
        in_specs=(
            P(None, "dp", None),
            P("dp", "opt"),
            P("dp", None),
            P("dp", "opt", None, None, None),
            P("dp", "opt", None, None, None),
            P("dp", "opt", None, None, None),
            P("dp", "opt", None, None, None),
        ),
        out_specs=(
            P("opt", "dp", None, None),
            P("dp", "opt", None, None, None),
            P("dp", "opt", None, None, None),
        ),
        check_vma=False,
    )
```

```python
import functools

import jax
import jax.numpy as jnp
from jax import lax
from jax.experimental import pallas as pl
from jax.experimental.pallas import tpu as pltpu
from jax.sharding import PartitionSpec as P

DECAY_RATE = 0.95
SIDE = 4
OFF = [(i, j) for i in range(4) for j in range(i + 1, 4)]
VMEM_BYTES = 20 * 1024 * 1024
EXTRA = 16
F32 = jnp.float32
BF16 = jnp.bfloat16


def params(limit=VMEM_BYTES):
    return pltpu.CompilerParams(vmem_limit_bytes=limit)


def cost(flops, moved):
    return pl.CostEstimate(flops=int(flops), bytes_accessed=int(moved), transcendentals=0)


def x_ring(step):
    return [(y * SIDE + x, y * SIDE + (x + step) % SIDE) for y in range(SIDE) for x in range(SIDE)]


def y_ring(step):
    return [(y * SIDE + x, ((y + step) % SIDE) * SIDE + x) for y in range(SIDE) for x in range(SIDE)]


def dot(a, b, over_a, over_b):
    return lax.dot_general(a, b, (((over_a,), (over_b,)), ((), ())), preferred_element_type=F32)


def partial_kernel(steps, place, source, target, *refs):
    count = (len(refs) - 4) // 2
    results, outs, (rows, cols, sems, out_sems) = refs[:count], refs[count : 2 * count], refs[2 * count :]
    block = cols.shape[1] // 2
    half = block // 2
    chooser, y, x = place[0], place[1], place[2]

    def units_of(r, along_x):
        for t in range(SIDE):
            k_y = lax.rem(y + (t if along_x else r), SIDE)
            k_x = lax.rem(x + (r if along_x else t), SIDE)
            row = (2 * k_y + lax.div(k_x, 2)) * block + (0 if along_x else half)
            yield t, pl.multiple_of(row, half), pl.multiple_of(lax.rem(k_x, 2) * block, block)

    def load(i, row):
        at = pl.ds(row, half)
        return pltpu.make_async_copy(source.at[chooser, :, at], rows.at[:, at], sems.at[i])

    first_x, first_y = x + steps[0], y + steps[0]
    plan = []
    for other in (0, 1):
        side = lax.rem(lax.div(lax.rem(first_x, SIDE), 2) + other, 2)
        for t in range(SIDE):
            plan.append((2 * lax.rem(y + t, SIDE) + side) * block)
        if len(steps) == 1:
            break
    upper = len(plan)
    for t in range(SIDE if len(steps) > 1 else 1):
        for side in range(2):
            plan.append((2 * lax.rem(first_y + t, SIDE) + side) * block + half)
    copies = [load(i, pl.multiple_of(row, half)) for i, row in enumerate(plan)]
    copies.append(pltpu.make_async_copy(target, cols, sems.at[len(plan)]))
    copies[-1].start()
    for copy in copies[:-1]:
        copy.start()
    copies[-1].wait()
    waited = [0]

    def wait_to(n):
        for copy in copies[waited[0] : n]:
            copy.wait()
        waited[0] = max(waited[0], n)

    leaving = []
    for along_x in (True, False):
        for n, r in enumerate(steps):
            o = 2 * n + (0 if along_x else 1)
            for i, (t, row, col) in enumerate(units_of(r, along_x)):
                if along_x:
                    wait_to(i + 1 if n == 0 else upper)
                else:
                    wait_to(upper + 2 if n == 0 else len(plan))
                outs[o][t] = dot(rows[:, pl.ds(row, half)], cols[:, pl.ds(col, block)], 0, 0).astype(BF16)
            leaving.append(pltpu.make_async_copy(outs[o], results[o], out_sems.at[o]))
            leaving[-1].start()
    wait_to(len(plan))
    for copy in leaving:
        copy.wait()


def partials(inputs, output_grads, place, steps, block):
    tok, feats = inputs.shape[1:]
    half = block // 2
    count = 2 * len(steps)
    units = SIDE * count
    shape = (SIDE, half, block)
    hbm = pl.BlockSpec(memory_space=pltpu.HBM)
    return pl.pallas_call(
        functools.partial(partial_kernel, steps),
        in_specs=[pl.BlockSpec(memory_space=pltpu.SMEM), hbm, hbm],
        out_specs=[hbm] * count,
        out_shape=[pltpu.HBM(shape, BF16)] * count,
        scratch_shapes=[pltpu.VMEM(shape, BF16)] * count
        + [
            pltpu.VMEM((tok, feats), BF16),
            pltpu.VMEM(output_grads.shape, BF16),
            pltpu.SemaphoreType.DMA((4 * SIDE + 1,)),
            pltpu.SemaphoreType.DMA((count,)),
        ],
        compiler_params=params(),
        cost_estimate=cost(
            2 * units * tok * half * block * 100,
            2 * (tok * feats + output_grads.size + units * half * block),
        ),
        name="partials",
    )(
        place,
        pltpu.with_memory_space_constraint(inputs, pltpu.HBM),
        pltpu.with_memory_space_constraint(output_grads, pltpu.HBM),
    )


def grid_masks(n):
    rows = lax.broadcasted_iota(jnp.int32, (n, n), 0)
    cols = lax.broadcasted_iota(jnp.int32, (n, n), 1)
    return rows, cols


def pack_kernel(left, right, out):
    q = left.shape[-1] // 4
    parts = out.shape[0]
    per = parts // 8
    step = q // per
    rows, cols = grid_masks(q)

    def put(slot, piece, value):
        for h in range(per):
            out[piece * per + h, slot * step : (slot + 1) * step] = value[h * step : (h + 1) * step]

    lines = []
    for c in range(left.shape[0]):
        for m, ref in enumerate((left, right)):

            def quarter(i, j, ref=ref, c=c):
                return ref[c, i * q : (i + 1) * q, j * q : (j + 1) * q]

            for n, (i, j) in enumerate(OFF):
                put(2 * c + m, n, quarter(i, j))
            for h in range(2):
                upper, lower = quarter(2 * h, 2 * h), quarter(2 * h + 1, 2 * h + 1)
                put(2 * c + m, len(OFF) + h, jnp.where(rows <= cols, upper, lower))
                lines.append(jnp.sum(jnp.where(rows == cols, lower.astype(F32), 0.0), axis=0, keepdims=True))
    lines.append(jnp.zeros((EXTRA - len(lines), q), F32))
    extra = jnp.concatenate(lines, axis=0).astype(BF16)
    for j in range(parts):
        out[j, 2 * left.shape[0] * step :] = extra


def pack_roots(left, right, parts):
    cap, block = left.shape[0], left.shape[-1]
    q = block // 4
    shape = (parts, 2 * cap * (8 * q // parts) + EXTRA, q)
    return pl.pallas_call(
        pack_kernel,
        out_shape=jax.ShapeDtypeStruct(shape, BF16),
        compiler_params=params(),
        cost_estimate=cost(0, 3 * 2 * left.size),
        name="pack_roots",
    )(left, right)


def pick_roots_kernel(slots, src, out):
    body = out.shape[1] - EXTRA
    cap = (src.shape[1] - EXTRA) // body
    for i in range(out.shape[0]):
        owner, rank = lax.div(slots[i], cap), lax.rem(slots[i], cap)
        out[i, :body] = src[owner, pl.ds(pl.multiple_of(rank * body, body), body)]
        out[i, body:] = src[owner, cap * body :]


def pick_roots(slots, src, cap):
    rows = (src.shape[1] - EXTRA) // cap + EXTRA
    return pl.pallas_call(
        pick_roots_kernel,
        in_specs=[pl.BlockSpec(memory_space=pltpu.SMEM), pl.BlockSpec(memory_space=pltpu.VMEM)],
        out_specs=pl.BlockSpec(memory_space=pltpu.VMEM),
        out_shape=jax.ShapeDtypeStruct((slots.shape[0], rows, src.shape[2]), src.dtype),
        compiler_params=params(),
        cost_estimate=cost(0, 4 * src.size),
        name="pick_roots",
    )(slots, src)


def pick_kernel(index, src, out):
    for i in range(out.shape[0]):
        at = index[i]

        @pl.when(at >= 0)
        def _(i=i, at=at):
            out[i] = src[jnp.maximum(at, 0)]

        @pl.when(at < 0)
        def _(i=i):
            out[i] = jnp.zeros(out.shape[1:], out.dtype)


def pick(index, src):
    shape = (index.shape[0],) + src.shape[1:]
    return pl.pallas_call(
        pick_kernel,
        in_specs=[pl.BlockSpec(memory_space=pltpu.SMEM), pl.BlockSpec(memory_space=pltpu.VMEM)],
        out_specs=pl.BlockSpec(memory_space=pltpu.VMEM),
        out_shape=jax.ShapeDtypeStruct(shape, src.dtype),
        compiler_params=params(),
        cost_estimate=cost(0, 4 * src.size),
        name="pick",
    )(index, src)


def unpack_kernel(ranks, packed, out):
    q = out.shape[-1] // 4
    per = packed.shape[0] // 8
    step = q // per
    rows, cols = grid_masks(q)
    rank = ranks[0]
    lines = packed[0, 2 * step :].astype(F32)
    for m in range(2):

        def piece(n, m=m):
            return jnp.concatenate([packed[n * per + h, m * step : (m + 1) * step] for h in range(per)], axis=0)

        def put(i, j, value, m=m):
            out[m, i * q : (i + 1) * q, j * q : (j + 1) * q] = value

        for n, (i, j) in enumerate(OFF):
            value = piece(n)
            put(i, j, value)
            put(j, i, value.T)
        for h in range(2):
            value = piece(len(OFF) + h)
            turned = value.T
            put(2 * h, 2 * h, jnp.where(rows <= cols, value, turned))
            own = lines[2 * m + h : 2 * m + h + 1, :]
            for c in range(1, (EXTRA // 4)):
                at = 4 * c + 2 * m + h
                own = jnp.where(rank == c, lines[at : at + 1, :], own)
            own = jnp.broadcast_to(own, (q, q)).astype(BF16)
            lower = jnp.where(rows > cols, value, turned)
            put(2 * h + 1, 2 * h + 1, jnp.where(rows == cols, own, lower))


def unpack_roots(rank, packed, block):
    return pl.pallas_call(
        unpack_kernel,
        in_specs=[pl.BlockSpec(memory_space=pltpu.SMEM), pl.BlockSpec(memory_space=pltpu.VMEM)],
        out_specs=pl.BlockSpec(memory_space=pltpu.VMEM),
        out_shape=jax.ShapeDtypeStruct((2, block, block), BF16),
        compiler_params=params(),
        cost_estimate=cost(0, 8 * block * block),
        name="unpack_roots",
    )(rank, packed)


def update_kernel(roots, grad, out):
    twisted = dot(grad[...], roots[1], 1, 0).astype(BF16)
    out[...] = dot(roots[0], twisted, 1, 0).astype(BF16)


def precondition(roots, grad):
    block = grad.shape[-1]
    return pl.pallas_call(
        update_kernel,
        out_shape=jax.ShapeDtypeStruct(grad.shape, BF16),
        compiler_params=params(),
        cost_estimate=cost(4 * block**3, 8 * block * block),
        name="precondition",
    )(roots, grad)


def gram_kernel(grads, left, right, left_out, right_out):
    block = left.shape[-1]
    grad = grads[...].reshape(block, block)
    gram = dot(grad, grad, 1, 1)
    left_out[...] = (left[...].astype(F32) * DECAY_RATE + gram / block).astype(BF16)
    gram = dot(grad, grad, 0, 0)
    right_out[...] = (right[...].astype(F32) * DECAY_RATE + gram / block).astype(BF16)


def grams(grads, left, right):
    parts, cap, rows, block = grads.shape
    stat = pl.BlockSpec((None, block, block), lambda c: (c, 0, 0))
    return pl.pallas_call(
        gram_kernel,
        grid=(cap,),
        in_specs=[pl.BlockSpec((parts, None, rows, block), lambda c: (0, c, 0, 0)), stat, stat],
        out_specs=[stat, stat],
        out_shape=[jax.ShapeDtypeStruct(left.shape, BF16)] * 2,
        compiler_params=params(),
        cost_estimate=cost(4 * cap * block**3, 10 * cap * block * block),
        name="grams",
    )(grads, *[pltpu.with_memory_space_constraint(a, pltpu.HBM) for a in (left, right)])


def total(*terms):
    return functools.reduce(jnp.add, [t.astype(F32) for t in terms]).astype(BF16)


def fold_kernel(*refs):
    terms, outs = refs[:SIDE], refs[SIDE:]
    for t, out in enumerate(outs):
        out[...] = total(*[term[t] for term in terms])


def fold(*terms):
    _, half, block = terms[0].shape
    return pl.pallas_call(
        fold_kernel,
        out_shape=[jax.ShapeDtypeStruct((half, block), BF16)] * SIDE,
        compiler_params=params(),
        cost_estimate=cost(0, 8 * half * block),
        name="fold",
    )(*terms)


def finish_kernel(*refs):
    refs[-1][...] = total(*[t[...] for t in refs[-1 - SIDE : -1]])


def finish(terms, at, rest=None):
    half, block = terms[0].shape
    spec = pl.BlockSpec((half, block), lambda i: (0, 0))
    return pl.pallas_call(
        finish_kernel,
        grid=(1,),
        in_specs=([] if rest is None else [pl.BlockSpec(memory_space=pl.ANY)]) + [spec] * SIDE,
        out_specs=pl.BlockSpec((half, block), lambda i: (at, 0)),
        out_shape=jax.ShapeDtypeStruct((2 * half, block), BF16),
        input_output_aliases={} if rest is None else {0: 0},
        compiler_params=params(),
        cost_estimate=cost(0, 10 * half * block),
        name="finish",
    )(*([] if rest is None else [rest]), *terms)


def shards(inputs, output_grads, owner_map, left_stats, right_stats, left_roots, right_roots):
    block = left_stats.shape[-1]
    cap = left_stats.shape[2]
    opt_count = lax.axis_size("opt")
    shard = lax.axis_index("opt")
    home = lax.axis_index("dp")
    chooser = (shard * 4 // opt_count == 3).astype(jnp.int32)
    place = jnp.stack([chooser, home // SIDE, home % SIDE])

    owners = owner_map[0]
    places = jnp.arange(opt_count, dtype=jnp.int32)
    same = (owners[None, :] == owners[:, None]) & (places[None, :] < places[:, None])
    slots = owners * cap + jnp.sum(same.astype(jnp.int32), axis=1)
    slot_ids = jnp.arange(opt_count * cap, dtype=jnp.int32)
    holders = slots[None, :] == slot_ids[:, None]
    homes = jnp.sum(jnp.where(holders, places[None, :] + 1, 0), axis=1) - 1

    a2, b2 = partials(inputs, output_grads, place, (2,), block)
    place, a2, b2 = lax.optimization_barrier((place, a2, b2))
    a1, b1, a3, b3, a0, b0 = partials(inputs, output_grads, place, (1, 3, 0), block)

    def send(value, ring):
        return lax.ppermute(value, "dp", ring)

    left_roots, right_roots, _ = lax.optimization_barrier((left_roots, right_roots, a2))
    packed = pack_roots(left_roots[0, 0], right_roots[0, 0], opt_count)
    spread = lax.all_to_all(packed, "opt", 0, 0, tiled=True)

    a_terms = [send(a2, x_ring(2)), send(a1, x_ring(1)), send(a3, x_ring(3))]
    b_terms = [send(b2, y_ring(2)), send(b1, y_ring(1)), send(b3, y_ring(3))]

    chosen = pick_roots(slots, spread, cap)
    a0, b0, _ = lax.optimization_barrier((a0, b0, chosen))
    a_terms, b_terms = lax.optimization_barrier((a_terms, b_terms))
    a_units, b_units = fold(a0, *a_terms), fold(b0, *b_terms)

    b_terms = [b_units[0]] + [send(b_units[t], x_ring(t)) for t in (2, 1, 3)]
    a_terms = [a_units[0]] + [send(a_units[t], y_ring(t)) for t in (2, 1, 3)]

    gathered = lax.all_to_all(chosen, "opt", 0, 0, tiled=True)
    rank = lax.dynamic_slice(slots, (shard,), (1,)) % cap
    roots = unpack_roots(rank, gathered, block)

    grad = finish(a_terms, 0, finish(b_terms, 1))
    grad, roots = lax.optimization_barrier((grad, roots))

    rows = block // opt_count
    spread = lax.all_to_all(grad.reshape(opt_count, rows, block), "opt", 0, 0, tiled=True)
    picked = pick(homes, spread).reshape(opt_count, cap, rows, block)
    owned = lax.all_to_all(picked, "opt", 0, 0, tiled=True)
    update = precondition(roots, grad)
    left_updated, right_updated = grams(owned, left_stats[0, 0], right_stats[0, 0])
    return update[None, None], left_updated[None, None], right_updated[None, None]


def solution(mesh):
    return jax.shard_map(
        shards,
        mesh=mesh,
        in_specs=(
            P(None, "dp", None),
            P("dp", "opt"),
            P("dp", None),
            P("dp", "opt", None, None, None),
            P("dp", "opt", None, None, None),
            P("dp", "opt", None, None, None),
            P("dp", "opt", None, None, None),
        ),
        out_specs=(
            P("opt", "dp", None, None),
            P("dp", "opt", None, None, None),
            P("dp", "opt", None, None, None),
        ),
        check_vma=False,
    )
```

```python
import functools

import jax
import jax.numpy as jnp
from jax import lax
from jax.experimental import pallas as pl
from jax.experimental.pallas import tpu as pltpu
from jax.sharding import PartitionSpec as P

DECAY_RATE = 0.95
SIDE = 4
OFF = [(i, j) for i in range(4) for j in range(i + 1, 4)]
VMEM_BYTES = 20 * 1024 * 1024
WEIGHT = 100
EXTRA = 16
F32 = jnp.float32
BF16 = jnp.bfloat16


def params(limit=VMEM_BYTES):
    return pltpu.CompilerParams(vmem_limit_bytes=limit)


def cost(flops, moved):
    return pl.CostEstimate(flops=int(flops), bytes_accessed=int(moved), transcendentals=0)


def x_ring(step):
    return [(y * SIDE + x, y * SIDE + (x + step) % SIDE) for y in range(SIDE) for x in range(SIDE)]


def y_ring(step):
    return [(y * SIDE + x, ((y + step) % SIDE) * SIDE + x) for y in range(SIDE) for x in range(SIDE)]


def dot(a, b, over_a, over_b):
    return lax.dot_general(a, b, (((over_a,), (over_b,)), ((), ())), preferred_element_type=F32)


def partial_kernel(steps, place, source, target, *refs):
    count = 2 * len(steps)
    extra = (len(refs) - 5 - 2 * count) // 2
    terms, results = refs[:extra], refs[extra : extra + count]
    held, outs = refs[extra + count : 2 * extra + count], refs[2 * extra + count : -5]
    rows, cols, sems, out_sems, term_sems = refs[-5:]
    block = cols.shape[1] // 2
    half = block // 2
    chooser, y, x = place[0], place[1], place[2]

    def units_of(r, along_x):
        for t in range(SIDE):
            k_y = lax.rem(y + (t if along_x else r), SIDE)
            k_x = lax.rem(x + (r if along_x else t), SIDE)
            row = (2 * k_y + lax.div(k_x, 2)) * block + (0 if along_x else half)
            yield t, pl.multiple_of(row, half), pl.multiple_of(lax.rem(k_x, 2) * block, block)

    def load(i, row):
        at = pl.ds(row, half)
        return pltpu.make_async_copy(source.at[chooser, :, at], rows.at[:, at], sems.at[i])

    plan = []
    for r in steps:
        side = lax.div(lax.rem(x + r, SIDE), 2)
        plan += [(2 * lax.rem(y + t, SIDE) + side) * block for t in range(SIDE)]
    upper = len(plan)
    for r in steps:
        plan += [(2 * lax.rem(y + r, SIDE) + side) * block + half for side in range(2)]
    copies = [load(i, pl.multiple_of(row, half)) for i, row in enumerate(plan)]
    copies.append(pltpu.make_async_copy(target, cols, sems.at[len(plan)]))
    copies[-1].start()
    for copy in copies[:-1]:
        copy.start()
    fetched = [pltpu.make_async_copy(term, held[o], term_sems.at[o]) for o, term in enumerate(terms)]
    for copy in fetched:
        copy.start()
    copies[-1].wait()
    waited = [0]

    def wait_to(n):
        for copy in copies[waited[0] : n]:
            copy.wait()
        waited[0] = max(waited[0], n)

    leaving = []
    for along_x in (True, False):
        for n, r in enumerate(steps):
            o = 2 * n + (0 if along_x else 1)
            for i, (t, row, col) in enumerate(units_of(r, along_x)):
                if along_x:
                    wait_to(SIDE * n + i + 1)
                else:
                    wait_to(upper + 2 * (n + 1))
                value = dot(rows[:, pl.ds(row, half)], cols[:, pl.ds(col, block)], 0, 0)
                if terms:
                    if t == 0:
                        fetched[o].wait()
                    value = value + held[o][t].astype(F32)
                outs[o][t] = value.astype(BF16)
            leaving.append(pltpu.make_async_copy(outs[o], results[o], out_sems.at[o]))
            leaving[-1].start()
    wait_to(len(plan))
    for copy in leaving:
        copy.wait()


def partials(inputs, output_grads, place, steps, block, terms=(), weight=1):
    tok, feats = inputs.shape[1:]
    half = block // 2
    count = 2 * len(steps)
    units = SIDE * count
    shape = (SIDE, half, block)
    hbm = pl.BlockSpec(memory_space=pltpu.HBM)
    return pl.pallas_call(
        functools.partial(partial_kernel, steps),
        in_specs=[pl.BlockSpec(memory_space=pltpu.SMEM)] + [hbm] * (2 + len(terms)),
        out_specs=[hbm] * count,
        out_shape=[pltpu.HBM(shape, BF16)] * count,
        scratch_shapes=[pltpu.VMEM(shape, BF16)] * (len(terms) + count)
        + [
            pltpu.VMEM((tok, feats), BF16),
            pltpu.VMEM(output_grads.shape, BF16),
            pltpu.SemaphoreType.DMA((4 * SIDE + 1,)),
            pltpu.SemaphoreType.DMA((count,)),
            pltpu.SemaphoreType.DMA((2,)),
        ],
        compiler_params=params(),
        cost_estimate=cost(
            2 * units * tok * half * block * weight,
            2 * (tok * feats + output_grads.size + units * half * block),
        ),
        name="partials",
    )(place, *[pltpu.with_memory_space_constraint(a, pltpu.HBM) for a in (inputs, output_grads, *terms)])


def grid_masks(n):
    rows = lax.broadcasted_iota(jnp.int32, (n, n), 0)
    cols = lax.broadcasted_iota(jnp.int32, (n, n), 1)
    return rows, cols


def pack_kernel(left, right, out):
    q = left.shape[-1] // 4
    parts = out.shape[0]
    per = parts // 8
    step = q // per
    rows, cols = grid_masks(q)

    def put(slot, piece, value):
        for h in range(per):
            out[piece * per + h, slot * step : (slot + 1) * step] = value[h * step : (h + 1) * step]

    lines = []
    for c in range(left.shape[0]):
        for m, ref in enumerate((left, right)):

            def quarter(i, j, ref=ref, c=c):
                return ref[c, i * q : (i + 1) * q, j * q : (j + 1) * q]

            for n, (i, j) in enumerate(OFF):
                put(2 * c + m, n, quarter(i, j))
            for h in range(2):
                upper, lower = quarter(2 * h, 2 * h), quarter(2 * h + 1, 2 * h + 1)
                put(2 * c + m, len(OFF) + h, jnp.where(rows <= cols, upper, lower))
                lines.append(jnp.sum(jnp.where(rows == cols, lower.astype(F32), 0.0), axis=0, keepdims=True))
    lines.append(jnp.zeros((EXTRA - len(lines), q), F32))
    extra = jnp.concatenate(lines, axis=0).astype(BF16)
    for j in range(parts):
        out[j, 2 * left.shape[0] * step :] = extra


def pack_roots(left, right, parts):
    cap, block = left.shape[0], left.shape[-1]
    q = block // 4
    shape = (parts, 2 * cap * (8 * q // parts) + EXTRA, q)
    return pl.pallas_call(
        pack_kernel,
        out_shape=jax.ShapeDtypeStruct(shape, BF16),
        compiler_params=params(),
        cost_estimate=cost(0, 3 * 2 * left.size),
        name="pack_roots",
    )(left, right)


def pick_roots_kernel(slots, src, out):
    body = out.shape[1] - EXTRA
    cap = (src.shape[1] - EXTRA) // body
    for i in range(out.shape[0]):
        owner, rank = lax.div(slots[i], cap), lax.rem(slots[i], cap)
        out[i, :body] = src[owner, pl.ds(pl.multiple_of(rank * body, body), body)]
        out[i, body:] = src[owner, cap * body :]


def pick_roots(slots, src, cap):
    rows = (src.shape[1] - EXTRA) // cap + EXTRA
    return pl.pallas_call(
        pick_roots_kernel,
        in_specs=[pl.BlockSpec(memory_space=pltpu.SMEM), pl.BlockSpec(memory_space=pltpu.VMEM)],
        out_specs=pl.BlockSpec(memory_space=pltpu.VMEM),
        out_shape=jax.ShapeDtypeStruct((slots.shape[0], rows, src.shape[2]), src.dtype),
        compiler_params=params(),
        cost_estimate=cost(0, 4 * src.size),
        name="pick_roots",
    )(slots, src)


def pick_kernel(index, src, out):
    for i in range(out.shape[0]):
        at = index[i]

        @pl.when(at >= 0)
        def _(i=i, at=at):
            out[i] = src[jnp.maximum(at, 0)]

        @pl.when(at < 0)
        def _(i=i):
            out[i] = jnp.zeros(out.shape[1:], out.dtype)


def pick(index, src):
    shape = (index.shape[0],) + src.shape[1:]
    return pl.pallas_call(
        pick_kernel,
        in_specs=[pl.BlockSpec(memory_space=pltpu.SMEM), pl.BlockSpec(memory_space=pltpu.VMEM)],
        out_specs=pl.BlockSpec(memory_space=pltpu.VMEM),
        out_shape=jax.ShapeDtypeStruct(shape, src.dtype),
        compiler_params=params(),
        cost_estimate=cost(0, 4 * src.size),
        name="pick",
    )(index, src)


def unpack_kernel(ranks, packed, out):
    q = out.shape[-1] // 4
    per = packed.shape[0] // 8
    step = q // per
    rows, cols = grid_masks(q)
    rank = ranks[0]
    lines = packed[0, 2 * step :].astype(F32)
    for m in range(2):

        def piece(n, m=m):
            return jnp.concatenate([packed[n * per + h, m * step : (m + 1) * step] for h in range(per)], axis=0)

        def put(i, j, value, m=m):
            out[m, i * q : (i + 1) * q, j * q : (j + 1) * q] = value

        for n, (i, j) in enumerate(OFF):
            value = piece(n)
            put(i, j, value)
            put(j, i, value.T)
        for h in range(2):
            value = piece(len(OFF) + h)
            turned = value.T
            put(2 * h, 2 * h, jnp.where(rows <= cols, value, turned))
            own = lines[2 * m + h : 2 * m + h + 1, :]
            for c in range(1, (EXTRA // 4)):
                at = 4 * c + 2 * m + h
                own = jnp.where(rank == c, lines[at : at + 1, :], own)
            own = jnp.broadcast_to(own, (q, q)).astype(BF16)
            lower = jnp.where(rows > cols, value, turned)
            put(2 * h + 1, 2 * h + 1, jnp.where(rows == cols, own, lower))


def unpack_roots(rank, packed, block):
    return pl.pallas_call(
        unpack_kernel,
        in_specs=[pl.BlockSpec(memory_space=pltpu.SMEM), pl.BlockSpec(memory_space=pltpu.VMEM)],
        out_specs=pl.BlockSpec(memory_space=pltpu.VMEM),
        out_shape=jax.ShapeDtypeStruct((2, block, block), BF16),
        compiler_params=params(),
        cost_estimate=cost(0, 8 * block * block),
        name="unpack_roots",
    )(rank, packed)


def update_kernel(roots, grad, out):
    twisted = dot(grad[...], roots[1], 1, 0).astype(BF16)
    out[...] = dot(roots[0], twisted, 1, 0).astype(BF16)


def precondition(roots, grad):
    block = grad.shape[-1]
    return pl.pallas_call(
        update_kernel,
        out_shape=jax.ShapeDtypeStruct(grad.shape, BF16),
        compiler_params=params(),
        cost_estimate=cost(4 * block**3, 8 * block * block),
        name="precondition",
    )(roots, grad)


def gram_kernel(grads, left, right, left_out, right_out):
    block = left.shape[-1]
    grad = grads[...].reshape(block, block)
    gram = dot(grad, grad, 1, 1)
    left_out[...] = (left[...].astype(F32) * DECAY_RATE + gram / block).astype(BF16)
    gram = dot(grad, grad, 0, 0)
    right_out[...] = (right[...].astype(F32) * DECAY_RATE + gram / block).astype(BF16)


def grams(grads, left, right):
    parts, cap, rows, block = grads.shape
    stat = pl.BlockSpec((None, block, block), lambda c: (c, 0, 0))
    return pl.pallas_call(
        gram_kernel,
        grid=(cap,),
        in_specs=[pl.BlockSpec((parts, None, rows, block), lambda c: (0, c, 0, 0)), stat, stat],
        out_specs=[stat, stat],
        out_shape=[jax.ShapeDtypeStruct(left.shape, BF16)] * 2,
        compiler_params=params(),
        cost_estimate=cost(4 * cap * block**3, 10 * cap * block * block),
        name="grams",
    )(grads, *[pltpu.with_memory_space_constraint(a, pltpu.HBM) for a in (left, right)])


def total(*terms):
    return functools.reduce(jnp.add, [t.astype(F32) for t in terms]).astype(BF16)


def fold_kernel(*refs):
    terms, outs = refs[:-SIDE], refs[-SIDE:]
    for t, out in enumerate(outs):
        out[...] = total(*[term[t] for term in terms])


def fold(own, *terms):
    _, half, block = own.shape
    return pl.pallas_call(
        fold_kernel,
        out_shape=[jax.ShapeDtypeStruct((half, block), BF16)] * SIDE,
        compiler_params=params(),
        cost_estimate=cost(0, 8 * half * block),
        name="fold",
    )(pltpu.with_memory_space_constraint(own, pltpu.HBM), *terms)


def finish_kernel(*refs):
    refs[-1][...] = total(*[t[...] for t in refs[-1 - SIDE : -1]])


def finish(terms, at, rest=None):
    half, block = terms[0].shape
    spec = pl.BlockSpec((half, block), lambda i: (0, 0))
    return pl.pallas_call(
        finish_kernel,
        grid=(1,),
        in_specs=([] if rest is None else [pl.BlockSpec(memory_space=pl.ANY)]) + [spec] * SIDE,
        out_specs=pl.BlockSpec((half, block), lambda i: (at, 0)),
        out_shape=jax.ShapeDtypeStruct((2 * half, block), BF16),
        input_output_aliases={} if rest is None else {0: 0},
        compiler_params=params(),
        cost_estimate=cost(0, 10 * half * block),
        name="finish",
    )(*([] if rest is None else [rest]), *terms)


def shards(inputs, output_grads, owner_map, left_stats, right_stats, left_roots, right_roots):
    block = left_stats.shape[-1]
    cap = left_stats.shape[2]
    opt_count = lax.axis_size("opt")
    shard = lax.axis_index("opt")
    home = lax.axis_index("dp")
    chooser = (shard * 4 // opt_count == 3).astype(jnp.int32)
    place = jnp.stack([chooser, home // SIDE, home % SIDE])

    owners = owner_map[0]
    places = jnp.arange(opt_count, dtype=jnp.int32)
    same = (owners[None, :] == owners[:, None]) & (places[None, :] < places[:, None])
    slots = owners * cap + jnp.sum(same.astype(jnp.int32), axis=1)
    slot_ids = jnp.arange(opt_count * cap, dtype=jnp.int32)
    holders = slots[None, :] == slot_ids[:, None]
    homes = jnp.sum(jnp.where(holders, places[None, :] + 1, 0), axis=1) - 1

    a2, b2 = partials(inputs, output_grads, place, (2,), block, weight=WEIGHT)
    place, a2, b2 = lax.optimization_barrier((place, a2, b2))
    a1, b1, a3, b3 = partials(inputs, output_grads, place, (1, 3), block, weight=WEIGHT)

    def send(value, ring):
        return lax.ppermute(value, "dp", ring)

    left_roots, right_roots, _ = lax.optimization_barrier((left_roots, right_roots, a2))
    packed = pack_roots(left_roots[0, 0], right_roots[0, 0], opt_count)
    spread = lax.all_to_all(packed, "opt", 0, 0, tiled=True)

    a_two, b_two = send(a2, x_ring(2)), send(b2, y_ring(2))
    a_terms = [send(a1, x_ring(1)), send(a3, x_ring(3))]
    b_terms = [send(b1, y_ring(1)), send(b3, y_ring(3))]
    a0, b0 = partials(inputs, output_grads, place, (0,), block, (a_two, b_two))

    spread, a0, b0 = lax.optimization_barrier((spread, a0, b0))
    chosen = pick_roots(slots, spread, cap)
    a_terms, b_terms, _ = lax.optimization_barrier((a_terms, b_terms, chosen))
    a_units, b_units = fold(a0, *a_terms), fold(b0, *b_terms)

    b_terms = [b_units[0]] + [send(b_units[t], x_ring(t)) for t in (2, 1, 3)]
    a_terms = [a_units[0]] + [send(a_units[t], y_ring(t)) for t in (2, 1, 3)]

    gathered = lax.all_to_all(chosen, "opt", 0, 0, tiled=True)
    rank = lax.dynamic_slice(slots, (shard,), (1,)) % cap
    roots = unpack_roots(rank, gathered, block)

    grad = finish(a_terms, 0, finish(b_terms, 1))
    grad, roots = lax.optimization_barrier((grad, roots))

    rows = block // opt_count
    spread = lax.all_to_all(grad.reshape(opt_count, rows, block), "opt", 0, 0, tiled=True)
    picked = pick(homes, spread).reshape(opt_count, cap, rows, block)
    owned = lax.all_to_all(picked, "opt", 0, 0, tiled=True)
    update = precondition(roots, grad)
    left_updated, right_updated = grams(owned, left_stats[0, 0], right_stats[0, 0])
    return update[None, None], left_updated[None, None], right_updated[None, None]


def solution(mesh):
    return jax.shard_map(
        shards,
        mesh=mesh,
        in_specs=(
            P(None, "dp", None),
            P("dp", "opt"),
            P("dp", None),
            P("dp", "opt", None, None, None),
            P("dp", "opt", None, None, None),
            P("dp", "opt", None, None, None),
            P("dp", "opt", None, None, None),
        ),
        out_specs=(
            P("opt", "dp", None, None),
            P("dp", "opt", None, None, None),
            P("dp", "opt", None, None, None),
        ),
        check_vma=False,
    )
```

```python
import functools

import jax
import jax.numpy as jnp
from jax import lax
from jax.experimental import pallas as pl
from jax.experimental.pallas import tpu as pltpu
from jax.sharding import PartitionSpec as P

DECAY_RATE = 0.95
SIDE = 4
OFF = [(i, j) for i in range(4) for j in range(i + 1, 4)]
VMEM_BYTES = 20 * 1024 * 1024
WEIGHT = 100
EXTRA = 16
F32 = jnp.float32
BF16 = jnp.bfloat16


def params(limit=VMEM_BYTES):
    return pltpu.CompilerParams(vmem_limit_bytes=limit)


def cost(flops, moved):
    return pl.CostEstimate(flops=int(flops), bytes_accessed=int(moved), transcendentals=0)


def x_ring(step):
    return [(y * SIDE + x, y * SIDE + (x + step) % SIDE) for y in range(SIDE) for x in range(SIDE)]


def y_ring(step):
    return [(y * SIDE + x, ((y + step) % SIDE) * SIDE + x) for y in range(SIDE) for x in range(SIDE)]


def dot(a, b, over_a, over_b):
    return lax.dot_general(a, b, (((over_a,), (over_b,)), ((), ())), preferred_element_type=F32)


def partial_kernel(steps, place, source, target, *refs):
    count = 2 * len(steps)
    extra = (len(refs) - 5 - 2 * count) // 2
    terms, results = refs[:extra], refs[extra : extra + count]
    held, outs = refs[extra + count : 2 * extra + count], refs[2 * extra + count : -5]
    rows, cols, sems, out_sems, term_sems = refs[-5:]
    block = cols.shape[1] // 2
    half = block // 2
    chooser, y, x = place[0], place[1], place[2]

    def units_of(r, along_x):
        for t in range(SIDE):
            k_y = lax.rem(y + (t if along_x else r), SIDE)
            k_x = lax.rem(x + (r if along_x else t), SIDE)
            row = (2 * k_y + lax.div(k_x, 2)) * block + (0 if along_x else half)
            yield t, pl.multiple_of(row, half), pl.multiple_of(lax.rem(k_x, 2) * block, block)

    def load(i, row):
        at = pl.ds(row, half)
        return pltpu.make_async_copy(source.at[chooser, :, at], rows.at[:, at], sems.at[i])

    plan = []
    for r in steps:
        side = lax.div(lax.rem(x + r, SIDE), 2)
        plan += [(2 * lax.rem(y + t, SIDE) + side) * block for t in range(SIDE)]
    upper = len(plan)
    for r in steps:
        plan += [(2 * lax.rem(y + r, SIDE) + side) * block + half for side in range(2)]
    copies = [load(i, pl.multiple_of(row, half)) for i, row in enumerate(plan)]
    side = lax.rem(x + steps[0], 2)
    halves = []
    for i in range(2):
        at = pl.ds(pl.multiple_of(lax.rem(side + i, 2) * block, block), block)
        halves.append(pltpu.make_async_copy(target.at[:, at], cols.at[:, at], sems.at[len(plan) + i]))
    halves[0].start()
    for copy in copies[:SIDE]:
        copy.start()
    halves[1].start()
    for copy in copies[SIDE:]:
        copy.start()
    fetched = [pltpu.make_async_copy(term, held[o], term_sems.at[o]) for o, term in enumerate(terms)]
    for copy in fetched:
        copy.start()
    halves[0].wait()
    waited = [0]

    def wait_to(n):
        for copy in copies[waited[0] : n]:
            copy.wait()
        waited[0] = max(waited[0], n)

    leaving = []
    for along_x in (True, False):
        if not along_x:
            halves[1].wait()
        for n, r in enumerate(steps):
            o = 2 * n + (0 if along_x else 1)
            for i, (t, row, col) in enumerate(units_of(r, along_x)):
                if along_x:
                    wait_to(SIDE * n + i + 1)
                else:
                    wait_to(upper + 2 * (n + 1))
                value = dot(rows[:, pl.ds(row, half)], cols[:, pl.ds(col, block)], 0, 0)
                if terms:
                    if t == 0:
                        fetched[o].wait()
                    value = value + held[o][t].astype(F32)
                outs[o][t] = value.astype(BF16)
            leaving.append(pltpu.make_async_copy(outs[o], results[o], out_sems.at[o]))
            leaving[-1].start()
    wait_to(len(plan))
    for copy in leaving:
        copy.wait()


def partials(inputs, output_grads, place, steps, block, terms=(), weight=1):
    tok, feats = inputs.shape[1:]
    half = block // 2
    count = 2 * len(steps)
    units = SIDE * count
    shape = (SIDE, half, block)
    hbm = pl.BlockSpec(memory_space=pltpu.HBM)
    return pl.pallas_call(
        functools.partial(partial_kernel, steps),
        in_specs=[pl.BlockSpec(memory_space=pltpu.SMEM)] + [hbm] * (2 + len(terms)),
        out_specs=[hbm] * count,
        out_shape=[pltpu.HBM(shape, BF16)] * count,
        scratch_shapes=[pltpu.VMEM(shape, BF16)] * (len(terms) + count)
        + [
            pltpu.VMEM((tok, feats), BF16),
            pltpu.VMEM(output_grads.shape, BF16),
            pltpu.SemaphoreType.DMA((4 * SIDE + 2,)),
            pltpu.SemaphoreType.DMA((count,)),
            pltpu.SemaphoreType.DMA((2,)),
        ],
        compiler_params=params(),
        cost_estimate=cost(
            2 * units * tok * half * block * weight,
            2 * (tok * feats + output_grads.size + units * half * block),
        ),
        name="partials",
    )(place, *[pltpu.with_memory_space_constraint(a, pltpu.HBM) for a in (inputs, output_grads, *terms)])


def grid_masks(n):
    rows = lax.broadcasted_iota(jnp.int32, (n, n), 0)
    cols = lax.broadcasted_iota(jnp.int32, (n, n), 1)
    return rows, cols


def pack_kernel(left, right, out):
    q = left.shape[-1] // 4
    parts = out.shape[0]
    per = parts // 8
    step = q // per
    rows, cols = grid_masks(q)

    def put(slot, piece, value):
        for h in range(per):
            out[piece * per + h, slot * step : (slot + 1) * step] = value[h * step : (h + 1) * step]

    lines = []
    for c in range(left.shape[0]):
        for m, ref in enumerate((left, right)):

            def quarter(i, j, ref=ref, c=c):
                return ref[c, i * q : (i + 1) * q, j * q : (j + 1) * q]

            for n, (i, j) in enumerate(OFF):
                put(2 * c + m, n, quarter(i, j))
            for h in range(2):
                upper, lower = quarter(2 * h, 2 * h), quarter(2 * h + 1, 2 * h + 1)
                put(2 * c + m, len(OFF) + h, jnp.where(rows <= cols, upper, lower))
                lines.append(jnp.sum(jnp.where(rows == cols, lower.astype(F32), 0.0), axis=0, keepdims=True))
    lines.append(jnp.zeros((EXTRA - len(lines), q), F32))
    extra = jnp.concatenate(lines, axis=0).astype(BF16)
    for j in range(parts):
        out[j, 2 * left.shape[0] * step :] = extra


def pack_roots(left, right, parts):
    cap, block = left.shape[0], left.shape[-1]
    q = block // 4
    shape = (parts, 2 * cap * (8 * q // parts) + EXTRA, q)
    return pl.pallas_call(
        pack_kernel,
        out_shape=jax.ShapeDtypeStruct(shape, BF16),
        compiler_params=params(),
        cost_estimate=cost(0, 3 * 2 * left.size),
        name="pack_roots",
    )(left, right)


def pick_roots_kernel(slots, src, out):
    body = out.shape[1] - EXTRA
    cap = (src.shape[1] - EXTRA) // body
    for i in range(out.shape[0]):
        owner, rank = lax.div(slots[i], cap), lax.rem(slots[i], cap)
        out[i, :body] = src[owner, pl.ds(pl.multiple_of(rank * body, body), body)]
        out[i, body:] = src[owner, cap * body :]


def pick_roots(slots, src, cap):
    rows = (src.shape[1] - EXTRA) // cap + EXTRA
    return pl.pallas_call(
        pick_roots_kernel,
        in_specs=[pl.BlockSpec(memory_space=pltpu.SMEM), pl.BlockSpec(memory_space=pltpu.VMEM)],
        out_specs=pl.BlockSpec(memory_space=pltpu.VMEM),
        out_shape=jax.ShapeDtypeStruct((slots.shape[0], rows, src.shape[2]), src.dtype),
        compiler_params=params(),
        cost_estimate=cost(0, 4 * src.size),
        name="pick_roots",
    )(slots, src)


def pick_kernel(index, src, out):
    for i in range(out.shape[0]):
        at = index[i]

        @pl.when(at >= 0)
        def _(i=i, at=at):
            out[i] = src[jnp.maximum(at, 0)]

        @pl.when(at < 0)
        def _(i=i):
            out[i] = jnp.zeros(out.shape[1:], out.dtype)


def pick(index, src):
    shape = (index.shape[0],) + src.shape[1:]
    return pl.pallas_call(
        pick_kernel,
        in_specs=[pl.BlockSpec(memory_space=pltpu.SMEM), pl.BlockSpec(memory_space=pltpu.VMEM)],
        out_specs=pl.BlockSpec(memory_space=pltpu.VMEM),
        out_shape=jax.ShapeDtypeStruct(shape, src.dtype),
        compiler_params=params(),
        cost_estimate=cost(0, 4 * src.size),
        name="pick",
    )(index, src)


def unpack_kernel(ranks, packed, out):
    q = out.shape[-1] // 4
    per = packed.shape[0] // 8
    step = q // per
    rows, cols = grid_masks(q)
    rank = ranks[0]
    lines = packed[0, 2 * step :].astype(F32)
    for m in range(2):

        def piece(n, m=m):
            return jnp.concatenate([packed[n * per + h, m * step : (m + 1) * step] for h in range(per)], axis=0)

        def put(i, j, value, m=m):
            out[m, i * q : (i + 1) * q, j * q : (j + 1) * q] = value

        for n, (i, j) in enumerate(OFF):
            value = piece(n)
            put(i, j, value)
            put(j, i, value.T)
        for h in range(2):
            value = piece(len(OFF) + h)
            turned = value.T
            put(2 * h, 2 * h, jnp.where(rows <= cols, value, turned))
            own = lines[2 * m + h : 2 * m + h + 1, :]
            for c in range(1, (EXTRA // 4)):
                at = 4 * c + 2 * m + h
                own = jnp.where(rank == c, lines[at : at + 1, :], own)
            own = jnp.broadcast_to(own, (q, q)).astype(BF16)
            lower = jnp.where(rows > cols, value, turned)
            put(2 * h + 1, 2 * h + 1, jnp.where(rows == cols, own, lower))


def unpack_roots(rank, packed, block):
    return pl.pallas_call(
        unpack_kernel,
        in_specs=[pl.BlockSpec(memory_space=pltpu.SMEM), pl.BlockSpec(memory_space=pltpu.VMEM)],
        out_specs=pl.BlockSpec(memory_space=pltpu.VMEM),
        out_shape=jax.ShapeDtypeStruct((2, block, block), BF16),
        compiler_params=params(),
        cost_estimate=cost(0, 8 * block * block),
        name="unpack_roots",
    )(rank, packed)


def update_kernel(roots, grad, out):
    twisted = dot(grad[...], roots[1], 1, 0).astype(BF16)
    out[...] = dot(roots[0], twisted, 1, 0).astype(BF16)


def precondition(roots, grad):
    block = grad.shape[-1]
    return pl.pallas_call(
        update_kernel,
        out_shape=jax.ShapeDtypeStruct(grad.shape, BF16),
        compiler_params=params(),
        cost_estimate=cost(4 * block**3, 8 * block * block),
        name="precondition",
    )(roots, grad)


def gram_kernel(grads, left, right, left_out, right_out):
    block = left.shape[-1]
    grad = grads[...].reshape(block, block)
    gram = dot(grad, grad, 1, 1)
    left_out[...] = (left[...].astype(F32) * DECAY_RATE + gram / block).astype(BF16)
    gram = dot(grad, grad, 0, 0)
    right_out[...] = (right[...].astype(F32) * DECAY_RATE + gram / block).astype(BF16)


def grams(grads, left, right):
    parts, cap, rows, block = grads.shape
    stat = pl.BlockSpec((None, block, block), lambda c: (c, 0, 0))
    return pl.pallas_call(
        gram_kernel,
        grid=(cap,),
        in_specs=[pl.BlockSpec((parts, None, rows, block), lambda c: (0, c, 0, 0)), stat, stat],
        out_specs=[stat, stat],
        out_shape=[jax.ShapeDtypeStruct(left.shape, BF16)] * 2,
        compiler_params=params(),
        cost_estimate=cost(4 * cap * block**3, 10 * cap * block * block),
        name="grams",
    )(grads, left, pltpu.with_memory_space_constraint(right, pltpu.HBM))


def total(*terms):
    return functools.reduce(jnp.add, [t.astype(F32) for t in terms]).astype(BF16)


def fold_kernel(*refs):
    terms, outs = refs[:-SIDE], refs[-SIDE:]
    for t, out in enumerate(outs):
        out[...] = total(*[term[t] for term in terms])


def fold(own, *terms):
    _, half, block = own.shape
    return pl.pallas_call(
        fold_kernel,
        out_shape=[jax.ShapeDtypeStruct((half, block), BF16)] * SIDE,
        compiler_params=params(),
        cost_estimate=cost(0, 8 * half * block),
        name="fold",
    )(pltpu.with_memory_space_constraint(own, pltpu.HBM), *terms)


def finish_kernel(*refs):
    refs[-1][...] = total(*[t[...] for t in refs[-1 - SIDE : -1]])


def finish(terms, at, rest=None):
    half, block = terms[0].shape
    spec = pl.BlockSpec((half, block), lambda i: (0, 0))
    return pl.pallas_call(
        finish_kernel,
        grid=(1,),
        in_specs=([] if rest is None else [pl.BlockSpec(memory_space=pl.ANY)]) + [spec] * SIDE,
        out_specs=pl.BlockSpec((half, block), lambda i: (at, 0)),
        out_shape=jax.ShapeDtypeStruct((2 * half, block), BF16),
        input_output_aliases={} if rest is None else {0: 0},
        compiler_params=params(),
        cost_estimate=cost(0, 10 * half * block),
        name="finish",
    )(*([] if rest is None else [rest]), *terms)


def shards(inputs, output_grads, owner_map, left_stats, right_stats, left_roots, right_roots):
    block = left_stats.shape[-1]
    cap = left_stats.shape[2]
    opt_count = lax.axis_size("opt")
    shard = lax.axis_index("opt")
    home = lax.axis_index("dp")
    chooser = (shard * 4 // opt_count == 3).astype(jnp.int32)
    place = jnp.stack([chooser, home // SIDE, home % SIDE])

    owners = owner_map[0]
    places = jnp.arange(opt_count, dtype=jnp.int32)
    same = (owners[None, :] == owners[:, None]) & (places[None, :] < places[:, None])
    slots = owners * cap + jnp.sum(same.astype(jnp.int32), axis=1)
    slot_ids = jnp.arange(opt_count * cap, dtype=jnp.int32)
    holders = slots[None, :] == slot_ids[:, None]
    homes = jnp.sum(jnp.where(holders, places[None, :] + 1, 0), axis=1) - 1

    a2, b2 = partials(inputs, output_grads, place, (2,), block, weight=WEIGHT)
    place, a2, b2 = lax.optimization_barrier((place, a2, b2))
    a1, b1, a3, b3 = partials(inputs, output_grads, place, (1, 3), block, weight=WEIGHT)

    def send(value, ring):
        return lax.ppermute(value, "dp", ring)

    left_roots, right_roots, _ = lax.optimization_barrier((left_roots, right_roots, a2))
    packed = pack_roots(left_roots[0, 0], right_roots[0, 0], opt_count)
    spread = lax.all_to_all(packed, "opt", 0, 0, tiled=True)

    a_two, b_two = send(a2, x_ring(2)), send(b2, y_ring(2))
    a_terms = [send(a1, x_ring(1)), send(a3, x_ring(3))]
    b_terms = [send(b1, y_ring(1)), send(b3, y_ring(3))]
    a0, b0 = partials(inputs, output_grads, place, (0,), block, (a_two, b_two))

    spread, a0, b0 = lax.optimization_barrier((spread, a0, b0))
    chosen = pick_roots(slots, spread, cap)
    a_terms, b_terms, _ = lax.optimization_barrier((a_terms, b_terms, chosen))
    a_units, b_units = fold(a0, *a_terms), fold(b0, *b_terms)

    b_terms = [b_units[0]] + [send(b_units[t], x_ring(t)) for t in (2, 1, 3)]
    a_terms = [a_units[0]] + [send(a_units[t], y_ring(t)) for t in (2, 1, 3)]

    gathered = lax.all_to_all(chosen, "opt", 0, 0, tiled=True)
    rank = lax.dynamic_slice(slots, (shard,), (1,)) % cap
    roots = unpack_roots(rank, gathered, block)

    grad = finish(a_terms, 0, finish(b_terms, 1))
    grad, roots = lax.optimization_barrier((grad, roots))

    rows = block // opt_count
    spread = lax.all_to_all(grad.reshape(opt_count, rows, block), "opt", 0, 0, tiled=True)
    picked = pick(homes, spread).reshape(opt_count, cap, rows, block)
    owned = lax.all_to_all(picked, "opt", 0, 0, tiled=True)
    update = precondition(roots, grad)
    left_updated, right_updated = grams(owned, left_stats[0, 0], right_stats[0, 0])
    return update[None, None], left_updated[None, None], right_updated[None, None]


def solution(mesh):
    return jax.shard_map(
        shards,
        mesh=mesh,
        in_specs=(
            P(None, "dp", None),
            P("dp", "opt"),
            P("dp", None),
            P("dp", "opt", None, None, None),
            P("dp", "opt", None, None, None),
            P("dp", "opt", None, None, None),
            P("dp", "opt", None, None, None),
        ),
        out_specs=(
            P("opt", "dp", None, None),
            P("dp", "opt", None, None, None),
            P("dp", "opt", None, None, None),
        ),
        check_vma=False,
    )
```

```python
import functools

import jax
import jax.numpy as jnp
from jax import lax
from jax.experimental import pallas as pl
from jax.experimental.pallas import tpu as pltpu
from jax.sharding import PartitionSpec as P

DECAY_RATE = 0.95
SIDE = 4
OFF = [(i, j) for i in range(4) for j in range(i + 1, 4)]
VMEM_BYTES = 20 * 1024 * 1024
WEIGHT = 100
EXTRA = 16
F32 = jnp.float32
BF16 = jnp.bfloat16


def params(limit=VMEM_BYTES):
    return pltpu.CompilerParams(vmem_limit_bytes=limit)


def cost(flops, moved):
    return pl.CostEstimate(flops=int(flops), bytes_accessed=int(moved), transcendentals=0)


def x_ring(step):
    return [(y * SIDE + x, y * SIDE + (x + step) % SIDE) for y in range(SIDE) for x in range(SIDE)]


def y_ring(step):
    return [(y * SIDE + x, ((y + step) % SIDE) * SIDE + x) for y in range(SIDE) for x in range(SIDE)]


def dot(a, b, over_a, over_b):
    return lax.dot_general(a, b, (((over_a,), (over_b,)), ((), ())), preferred_element_type=F32)


def position():
    home = lax.axis_index("dp")
    fourth = lax.div(lax.axis_index("opt") * 4, lax.axis_size("opt"))
    return (fourth == 3).astype(jnp.int32), lax.div(home, SIDE), lax.rem(home, SIDE)


def partial_kernel(steps, inside, place, source, target, *refs):
    count = 2 * len(steps)
    extra = (len(refs) - 5 - 2 * count) // 2
    terms, results = refs[:extra], refs[extra : extra + count]
    held, outs = refs[extra + count : 2 * extra + count], refs[2 * extra + count : -5]
    rows, cols, sems, out_sems, term_sems = refs[-5:]
    block = cols.shape[1] // 2
    half = block // 2
    chooser, y, x = position() if inside else (place[0], place[1], place[2])

    def units_of(r, along_x):
        for t in range(SIDE):
            k_y = lax.rem(y + (t if along_x else r), SIDE)
            k_x = lax.rem(x + (r if along_x else t), SIDE)
            row = (2 * k_y + lax.div(k_x, 2)) * block + (0 if along_x else half)
            yield t, pl.multiple_of(row, half), pl.multiple_of(lax.rem(k_x, 2) * block, block)

    def load(i, row):
        at = pl.ds(row, half)
        return pltpu.make_async_copy(source.at[chooser, :, at], rows.at[:, at], sems.at[i])

    plan = []
    for r in steps:
        side = lax.div(lax.rem(x + r, SIDE), 2)
        plan += [(2 * lax.rem(y + t, SIDE) + side) * block for t in range(SIDE)]
    upper = len(plan)
    for r in steps:
        plan += [(2 * lax.rem(y + r, SIDE) + side) * block + half for side in range(2)]
    copies = [load(i, pl.multiple_of(row, half)) for i, row in enumerate(plan)]
    side = lax.rem(x + steps[0], 2)
    halves = []
    for i in range(2):
        at = pl.ds(pl.multiple_of(lax.rem(side + i, 2) * block, block), block)
        halves.append(pltpu.make_async_copy(target.at[:, at], cols.at[:, at], sems.at[len(plan) + i]))
    halves[0].start()
    for copy in copies[:SIDE]:
        copy.start()
    halves[1].start()
    for copy in copies[SIDE:]:
        copy.start()
    fetched = [pltpu.make_async_copy(term, held[o], term_sems.at[o]) for o, term in enumerate(terms)]
    for copy in fetched:
        copy.start()
    halves[0].wait()
    waited = [0]

    def wait_to(n):
        for copy in copies[waited[0] : n]:
            copy.wait()
        waited[0] = max(waited[0], n)

    leaving = []
    for along_x in (True, False):
        if not along_x:
            halves[1].wait()
        for n, r in enumerate(steps):
            o = 2 * n + (0 if along_x else 1)
            for i, (t, row, col) in enumerate(units_of(r, along_x)):
                if along_x:
                    wait_to(SIDE * n + i + 1)
                else:
                    wait_to(upper + 2 * (n + 1))
                value = dot(rows[:, pl.ds(row, half)], cols[:, pl.ds(col, block)], 0, 0)
                if terms:
                    if t == 0:
                        fetched[o].wait()
                    value = value + held[o][t].astype(F32)
                outs[o][t] = value.astype(BF16)
            leaving.append(pltpu.make_async_copy(outs[o], results[o], out_sems.at[o]))
            leaving[-1].start()
    wait_to(len(plan))
    for copy in leaving:
        copy.wait()


def partials(inputs, output_grads, place, steps, block, terms=(), weight=1):
    tok, feats = inputs.shape[1:]
    half = block // 2
    count = 2 * len(steps)
    units = SIDE * count
    shape = (SIDE, half, block)
    hbm = pl.BlockSpec(memory_space=pltpu.HBM)
    return pl.pallas_call(
        functools.partial(partial_kernel, steps, place is None),
        in_specs=[pl.BlockSpec(memory_space=pltpu.SMEM)] + [hbm] * (2 + len(terms)),
        out_specs=[hbm] * count,
        out_shape=[pltpu.HBM(shape, BF16)] * count,
        scratch_shapes=[pltpu.VMEM(shape, BF16)] * (len(terms) + count)
        + [
            pltpu.VMEM((tok, feats), BF16),
            pltpu.VMEM(output_grads.shape, BF16),
            pltpu.SemaphoreType.DMA((4 * SIDE + 2,)),
            pltpu.SemaphoreType.DMA((count,)),
            pltpu.SemaphoreType.DMA((2,)),
        ],
        compiler_params=params(),
        cost_estimate=cost(
            2 * units * tok * half * block * weight,
            2 * (tok * feats + output_grads.size + units * half * block),
        ),
        name="partials",
    )(jnp.zeros((3,), jnp.int32) if place is None else place, *[pltpu.with_memory_space_constraint(a, pltpu.HBM) for a in (inputs, output_grads, *terms)])


def grid_masks(n):
    rows = lax.broadcasted_iota(jnp.int32, (n, n), 0)
    cols = lax.broadcasted_iota(jnp.int32, (n, n), 1)
    return rows, cols


def pack_kernel(left, right, out):
    q = left.shape[-1] // 4
    parts = out.shape[0]
    per = parts // 8
    step = q // per
    rows, cols = grid_masks(q)

    def put(slot, piece, value):
        for h in range(per):
            out[piece * per + h, slot * step : (slot + 1) * step] = value[h * step : (h + 1) * step]

    lines = []
    for c in range(left.shape[0]):
        for m, ref in enumerate((left, right)):

            def quarter(i, j, ref=ref, c=c):
                return ref[c, i * q : (i + 1) * q, j * q : (j + 1) * q]

            for n, (i, j) in enumerate(OFF):
                put(2 * c + m, n, quarter(i, j))
            for h in range(2):
                upper, lower = quarter(2 * h, 2 * h), quarter(2 * h + 1, 2 * h + 1)
                put(2 * c + m, len(OFF) + h, jnp.where(rows <= cols, upper, lower))
                lines.append(jnp.sum(jnp.where(rows == cols, lower.astype(F32), 0.0), axis=0, keepdims=True))
    lines.append(jnp.zeros((EXTRA - len(lines), q), F32))
    extra = jnp.concatenate(lines, axis=0).astype(BF16)
    for j in range(parts):
        out[j, 2 * left.shape[0] * step :] = extra


def pack_roots(left, right, parts):
    cap, block = left.shape[0], left.shape[-1]
    q = block // 4
    shape = (parts, 2 * cap * (8 * q // parts) + EXTRA, q)
    return pl.pallas_call(
        pack_kernel,
        out_shape=jax.ShapeDtypeStruct(shape, BF16),
        compiler_params=params(),
        cost_estimate=cost(0, 3 * 2 * left.size),
        name="pack_roots",
    )(left, right)


def pick_roots_kernel(slots, src, out):
    body = out.shape[1] - EXTRA
    cap = (src.shape[1] - EXTRA) // body
    for i in range(out.shape[0]):
        owner, rank = lax.div(slots[i], cap), lax.rem(slots[i], cap)
        out[i, :body] = src[owner, pl.ds(pl.multiple_of(rank * body, body), body)]
        out[i, body:] = src[owner, cap * body :]


def pick_roots(slots, src, cap):
    rows = (src.shape[1] - EXTRA) // cap + EXTRA
    return pl.pallas_call(
        pick_roots_kernel,
        in_specs=[pl.BlockSpec(memory_space=pltpu.SMEM), pl.BlockSpec(memory_space=pltpu.VMEM)],
        out_specs=pl.BlockSpec(memory_space=pltpu.VMEM),
        out_shape=jax.ShapeDtypeStruct((slots.shape[0], rows, src.shape[2]), src.dtype),
        compiler_params=params(),
        cost_estimate=cost(0, 4 * src.size),
        name="pick_roots",
    )(slots, src)


def pick_kernel(index, src, out):
    for i in range(out.shape[0]):
        at = index[i]

        @pl.when(at >= 0)
        def _(i=i, at=at):
            out[i] = src[jnp.maximum(at, 0)]

        @pl.when(at < 0)
        def _(i=i):
            out[i] = jnp.zeros(out.shape[1:], out.dtype)


def pick(index, src):
    shape = (index.shape[0],) + src.shape[1:]
    return pl.pallas_call(
        pick_kernel,
        in_specs=[pl.BlockSpec(memory_space=pltpu.SMEM), pl.BlockSpec(memory_space=pltpu.VMEM)],
        out_specs=pl.BlockSpec(memory_space=pltpu.VMEM),
        out_shape=jax.ShapeDtypeStruct(shape, src.dtype),
        compiler_params=params(),
        cost_estimate=cost(0, 4 * src.size),
        name="pick",
    )(index, src)


def unpack_kernel(ranks, packed, out):
    q = out.shape[-1] // 4
    per = packed.shape[0] // 8
    step = q // per
    rows, cols = grid_masks(q)
    rank = ranks[0]
    lines = packed[0, 2 * step :].astype(F32)
    for m in range(2):

        def piece(n, m=m):
            return jnp.concatenate([packed[n * per + h, m * step : (m + 1) * step] for h in range(per)], axis=0)

        def put(i, j, value, m=m):
            out[m, i * q : (i + 1) * q, j * q : (j + 1) * q] = value

        for n, (i, j) in enumerate(OFF):
            value = piece(n)
            put(i, j, value)
            put(j, i, value.T)
        for h in range(2):
            value = piece(len(OFF) + h)
            turned = value.T
            put(2 * h, 2 * h, jnp.where(rows <= cols, value, turned))
            own = lines[2 * m + h : 2 * m + h + 1, :]
            for c in range(1, (EXTRA // 4)):
                at = 4 * c + 2 * m + h
                own = jnp.where(rank == c, lines[at : at + 1, :], own)
            own = jnp.broadcast_to(own, (q, q)).astype(BF16)
            lower = jnp.where(rows > cols, value, turned)
            put(2 * h + 1, 2 * h + 1, jnp.where(rows == cols, own, lower))


def unpack_roots(rank, packed, block):
    return pl.pallas_call(
        unpack_kernel,
        in_specs=[pl.BlockSpec(memory_space=pltpu.SMEM), pl.BlockSpec(memory_space=pltpu.VMEM)],
        out_specs=pl.BlockSpec(memory_space=pltpu.VMEM),
        out_shape=jax.ShapeDtypeStruct((2, block, block), BF16),
        compiler_params=params(),
        cost_estimate=cost(0, 8 * block * block),
        name="unpack_roots",
    )(rank, packed)


def update_kernel(roots, grad, out):
    twisted = dot(grad[...], roots[1], 1, 0).astype(BF16)
    out[...] = dot(roots[0], twisted, 1, 0).astype(BF16)


def precondition(roots, grad):
    block = grad.shape[-1]
    return pl.pallas_call(
        update_kernel,
        out_shape=jax.ShapeDtypeStruct(grad.shape, BF16),
        compiler_params=params(),
        cost_estimate=cost(4 * block**3, 8 * block * block),
        name="precondition",
    )(roots, grad)


def gram_kernel(grads, left, right, left_out, right_out):
    block = left.shape[-1]
    grad = grads[...].reshape(block, block)
    gram = dot(grad, grad, 1, 1)
    left_out[...] = (left[...].astype(F32) * DECAY_RATE + gram / block).astype(BF16)
    gram = dot(grad, grad, 0, 0)
    right_out[...] = (right[...].astype(F32) * DECAY_RATE + gram / block).astype(BF16)


def grams(grads, left, right):
    parts, cap, rows, block = grads.shape
    stat = pl.BlockSpec((None, block, block), lambda c: (c, 0, 0))
    return pl.pallas_call(
        gram_kernel,
        grid=(cap,),
        in_specs=[pl.BlockSpec((parts, None, rows, block), lambda c: (0, c, 0, 0)), stat, stat],
        out_specs=[stat, stat],
        out_shape=[jax.ShapeDtypeStruct(left.shape, BF16)] * 2,
        compiler_params=params(),
        cost_estimate=cost(4 * cap * block**3, 10 * cap * block * block),
        name="grams",
    )(grads, left, pltpu.with_memory_space_constraint(right, pltpu.HBM))


def total(*terms):
    return functools.reduce(jnp.add, [t.astype(F32) for t in terms]).astype(BF16)


def fold_kernel(*refs):
    terms, outs = refs[:-SIDE], refs[-SIDE:]
    for t, out in enumerate(outs):
        out[...] = total(*[term[t] for term in terms])


def fold(own, *terms):
    _, half, block = own.shape
    return pl.pallas_call(
        fold_kernel,
        out_shape=[jax.ShapeDtypeStruct((half, block), BF16)] * SIDE,
        compiler_params=params(),
        cost_estimate=cost(0, 8 * half * block),
        name="fold",
    )(pltpu.with_memory_space_constraint(own, pltpu.HBM), *terms)


def finish_kernel(*refs):
    refs[-1][...] = total(*[t[...] for t in refs[-1 - SIDE : -1]])


def finish(terms, at, rest=None):
    half, block = terms[0].shape
    spec = pl.BlockSpec((half, block), lambda i: (0, 0))
    return pl.pallas_call(
        finish_kernel,
        grid=(1,),
        in_specs=([] if rest is None else [pl.BlockSpec(memory_space=pl.ANY)]) + [spec] * SIDE,
        out_specs=pl.BlockSpec((half, block), lambda i: (at, 0)),
        out_shape=jax.ShapeDtypeStruct((2 * half, block), BF16),
        input_output_aliases={} if rest is None else {0: 0},
        compiler_params=params(),
        cost_estimate=cost(0, 10 * half * block),
        name="finish",
    )(*([] if rest is None else [rest]), *terms)


def shards(inputs, output_grads, owner_map, left_stats, right_stats, left_roots, right_roots):
    block = left_stats.shape[-1]
    cap = left_stats.shape[2]
    opt_count = lax.axis_size("opt")
    shard = lax.axis_index("opt")
    place = jnp.stack(position())

    owners = owner_map[0]
    places = jnp.arange(opt_count, dtype=jnp.int32)
    same = (owners[None, :] == owners[:, None]) & (places[None, :] < places[:, None])
    slots = owners * cap + jnp.sum(same.astype(jnp.int32), axis=1)
    slot_ids = jnp.arange(opt_count * cap, dtype=jnp.int32)
    holders = slots[None, :] == slot_ids[:, None]
    homes = jnp.sum(jnp.where(holders, places[None, :] + 1, 0), axis=1) - 1

    a2, b2 = partials(inputs, output_grads, None, (2,), block, weight=WEIGHT)
    place, a2, b2 = lax.optimization_barrier((place, a2, b2))
    a1, b1, a3, b3 = partials(inputs, output_grads, place, (1, 3), block, weight=WEIGHT)

    def send(value, ring):
        return lax.ppermute(value, "dp", ring)

    left_roots, right_roots, _ = lax.optimization_barrier((left_roots, right_roots, a2))
    packed = pack_roots(left_roots[0, 0], right_roots[0, 0], opt_count)
    spread = lax.all_to_all(packed, "opt", 0, 0, tiled=True)

    a_two, b_two = send(a2, x_ring(2)), send(b2, y_ring(2))
    a_terms = [send(a1, x_ring(1)), send(a3, x_ring(3))]
    b_terms = [send(b1, y_ring(1)), send(b3, y_ring(3))]
    a0, b0 = partials(inputs, output_grads, place, (0,), block, (a_two, b_two))

    spread, a0, b0 = lax.optimization_barrier((spread, a0, b0))
    chosen = pick_roots(slots, spread, cap)
    a_terms, b_terms, _ = lax.optimization_barrier((a_terms, b_terms, chosen))
    a_units, b_units = fold(a0, *a_terms), fold(b0, *b_terms)

    b_terms = [b_units[0]] + [send(b_units[t], x_ring(t)) for t in (2, 1, 3)]
    a_terms = [a_units[0]] + [send(a_units[t], y_ring(t)) for t in (2, 1, 3)]

    gathered = lax.all_to_all(chosen, "opt", 0, 0, tiled=True)
    rank = lax.dynamic_slice(slots, (shard,), (1,)) % cap
    roots = unpack_roots(rank, gathered, block)

    grad = finish(a_terms, 0, finish(b_terms, 1))
    grad, roots = lax.optimization_barrier((grad, roots))

    rows = block // opt_count
    spread = lax.all_to_all(grad.reshape(opt_count, rows, block), "opt", 0, 0, tiled=True)
    picked = pick(homes, spread).reshape(opt_count, cap, rows, block)
    owned = lax.all_to_all(picked, "opt", 0, 0, tiled=True)
    update = precondition(roots, grad)
    left_updated, right_updated = grams(owned, left_stats[0, 0], right_stats[0, 0])
    return update[None, None], left_updated[None, None], right_updated[None, None]


def solution(mesh):
    return jax.shard_map(
        shards,
        mesh=mesh,
        in_specs=(
            P(None, "dp", None),
            P("dp", "opt"),
            P("dp", None),
            P("dp", "opt", None, None, None),
            P("dp", "opt", None, None, None),
            P("dp", "opt", None, None, None),
            P("dp", "opt", None, None, None),
        ),
        out_specs=(
            P("opt", "dp", None, None),
            P("dp", "opt", None, None, None),
            P("dp", "opt", None, None, None),
        ),
        check_vma=False,
    )
```
